256 devices in a mesh: src: 16 (over z_lo, y, core), rcv: 16 (over x, z_hi).
Axes of the slice: x: 4, y: 4, z: 8 (z_hi: 4, z_lo: 2; z = z_hi * 2 + z_lo), core: 2. Of those that a mesh axis runs over, the one named last changes fastest.
Arguments:
- traces: bfloat16 [512, 512, 512], P('src', 'rcv'), may hold values from -6 to 6
- dead_mask: int32 [512, 512], P('src', 'rcv'), may hold values 0 or 1
- filters: bfloat16 [512, 256], P(('src', 'rcv')), may hold values from -0.375 to 0.375
- station_of_slot: int32 [512], replicated, may hold values from 0 to 511, each once
Outputs:
- residual: bfloat16 [512, 512, 512], P('src', 'rcv')
- grad_receiver: float32 [512, 256], P('rcv')
- grad_source: float32 [512, 256], P('src')
The draws below stay inside these ranges and needn't reach their ends.
Inputs may be any that keep to these rules, and one draw needn't show every extreme that they name: `station_of_slot`: every station number stands in exactly one slot. `dead_mask`: 1 marks a live trace, 0 a dead one.
All inputs are finite; a program needn't handle non-finite values. No bound on the sum of `dead_mask` on one device may be relied on, other than what follows from the above.
Results may differ from the reference program's by a relative error of at most 0.014.
Values may be sent and summed in bfloat16 or wider, within the bound.
A program may use at most 64 MiB of HBM per device.

```python
import math
import jax
import jax.numpy as jnp
from jax import lax

NT = 512
TAPS = 256
FINE = 2
STATIONS = 512
SRC_BLOCK = 32
RCV_BLOCK = 32
N_SRC = 16
N_RCV = 16


def place_ends(array, stream_key, least, high):
    extent = array.shape
    index_at = [jax.random.randint(jax.random.fold_in(stream_key, axis), (), 0, extent[axis]) for axis in range(len(extent))]
    array = array.at[tuple(index_at)].set(least)
    longest = extent.index(max(extent))
    index_at[longest] = (index_at[longest] + 1) % extent[longest]
    return array.at[tuple(index_at)].set(high)


def steps_of(key, dims, split, smallest, high):
    def one(axis_at, blocks):
        steps = jax.random.uniform(jax.random.fold_in(jax.random.fold_in(key, 6), axis_at), (blocks,), jnp.float32, smallest / len(split), high / len(split))
        return jnp.repeat(jnp.exp(steps), dims[axis_at] // blocks).reshape((-1,) + (1,) * (len(dims) - axis_at - 1))

    loudness = one(*split[0])
    for cut in split[1:]:
        loudness = loudness * one(*cut)
    return loudness


def noise(key, extent, width, reach, shards=(), kind=jnp.bfloat16):
    entries = jax.random.normal(key, extent, jnp.float32) * width
    if len(shards) > 0:
        entries = steps_of(key, extent, shards, -0.22, 0.18) * entries
    return jnp.clip(entries, min=-reach, max=reach).astype(kind)


def setup_inputs(seed: int = 0) -> dict:
    arg_keys = jax.random.split(jax.random.key(seed), 5)
    return {
        "traces": noise(arg_keys[0], (STATIONS, STATIONS, NT), 1.0, 6.0, ((0, 16), (1, 16))),
        "dead_mask": place_ends((jax.random.randint(arg_keys[1], (STATIONS, STATIONS), 0, 8) < 7).astype(jnp.int32), jax.random.fold_in(arg_keys[1], 1), 0, 1),
        "filters": noise(arg_keys[2], (STATIONS, TAPS), TAPS ** -0.5, 0.375, ((0, 256),)),
        "station_of_slot": jax.random.permutation(arg_keys[3], STATIONS).astype(jnp.int32),
    }


def reference(traces, dead_mask, filters, station_of_slot):
    fft_length = NT + TAPS
    column_ids = jnp.arange(STATIONS, dtype=jnp.int32)
    within_block = column_ids % RCV_BLOCK
    column_slot = (within_block // FINE * N_RCV + column_ids // RCV_BLOCK) * FINE + within_block % FINE
    slot_ids = jnp.arange(STATIONS, dtype=jnp.int32)
    slot_group = slot_ids // FINE
    column_of_slot = slot_group % N_RCV * RCV_BLOCK + slot_group // N_RCV * FINE + slot_ids % FINE
    slot_taps = filters.astype(jnp.float32)[station_of_slot]
    column_spectra = jnp.fft.rfft(slot_taps[column_slot], n=fft_length, axis=-1)
    shuffled = traces[column_slot]
    scale = 1.0 / math.sqrt(STATIONS * NT)

    def one_block(carried, begin_at):
        row_traces = lax.dynamic_slice_in_dim(traces, begin_at, SRC_BLOCK, 0).astype(jnp.float32)
        row_live = lax.dynamic_slice_in_dim(dead_mask, begin_at, SRC_BLOCK, 0).astype(jnp.float32)
        picked = lax.dynamic_slice_in_dim(column_of_slot, begin_at, SRC_BLOCK, 0)
        mirror = jnp.swapaxes(jnp.take(shuffled, picked, axis=1), 0, 1).astype(jnp.float32)
        row_spectra = jnp.fft.rfft(lax.dynamic_slice_in_dim(slot_taps, begin_at, SRC_BLOCK, 0), n=fft_length, axis=-1)
        trace_spectra = jnp.fft.rfft(row_traces, n=fft_length, axis=-1)
        mirror_spectra = jnp.fft.rfft(mirror, n=fft_length, axis=-1)
        column_filtered = jnp.fft.irfft(trace_spectra * column_spectra[None], n=fft_length, axis=-1)[..., :NT].astype(jnp.bfloat16)
        row_filtered = jnp.fft.irfft(mirror_spectra * row_spectra[:, None], n=fft_length, axis=-1)[..., :NT].astype(jnp.bfloat16)
        residual = (row_live[..., None] * (column_filtered.astype(jnp.float32) - row_filtered.astype(jnp.float32))).astype(jnp.bfloat16)
        residual_spectra = jnp.fft.rfft(residual.astype(jnp.float32), n=fft_length, axis=-1)
        receiver_part = jnp.fft.irfft(lax.optimization_barrier(jnp.sum(residual_spectra * jnp.conj(trace_spectra), axis=0)), n=fft_length, axis=-1)[:, :TAPS]
        source_part = -jnp.fft.irfft(lax.optimization_barrier(jnp.sum(residual_spectra * jnp.conj(mirror_spectra), axis=1)), n=fft_length, axis=-1)[:, :TAPS]
        return (carried + receiver_part, (residual, source_part))
    begins = jnp.arange(N_SRC, dtype=jnp.int32) * SRC_BLOCK
    receiver_total, stacked = lax.scan(one_block, jnp.zeros((STATIONS, TAPS), jnp.float32), begins)
    residual = stacked[0].reshape(STATIONS, STATIONS, NT)
    grad_source = stacked[1].reshape(STATIONS, TAPS) * scale
    grad_receiver = receiver_total * scale
    return (residual, grad_receiver, grad_source)
```

```python
import functools
import math

import jax
import jax.numpy as jnp
from jax import lax
from jax.experimental import pallas as pl
from jax.experimental.pallas import tpu as pltpu
from jax.sharding import PartitionSpec as P

MESH = pl.DeviceIdType.MESH
station_group = 4


def digits_of(n_src, n_rcv):
    if (n_src, n_rcv) == (16, 16):
        return (2, 4, 2), (4, 4)
    return (1, n_src // 2, 2), (n_rcv // 2, 2)


def line_peers(S, R, n_src, n_rcv):
    (nl, ny, nc), (nx, nh) = digits_of(n_src, n_rcv)
    l, y, c = S // (ny * nc), lax.rem(S // nc, ny), lax.rem(S, nc)
    x, h = R // nh, lax.rem(R, nh)

    def at(dl, dy, dc, dx, dh):
        s = (lax.rem(l + dl, nl) * ny + lax.rem(y + dy, ny)) * nc + lax.rem(c + dc, nc)
        return s, lax.rem(x + dx, nx) * nh + lax.rem(h + dh, nh)

    z = [at(a, 0, 0, 0, b) for a in range(nl) for b in range(nh) if a or b]
    xs = [at(0, 0, 0, a, 0) for a in range(1, nx)]
    ys = [at(0, a, 0, 0, 0) for a in range(1, ny)]
    cs = [at(0, 0, a, 0, 0) for a in range(1, nc)]
    return z, xs, ys, cs


def enter(S, R, n_src, n_rcv, stage_sems):
    z, xs, ys, cs = line_peers(S, R, n_src, n_rcv)
    bar = pltpu.get_barrier_semaphore()
    near = z + xs + ys + cs
    for d in near:
        pl.semaphore_signal(bar, inc=1, device_id=d, device_id_type=MESH)
    pl.semaphore_wait(bar, len(near))
    for i, group in enumerate((xs, ys, cs)):
        for d in group:
            pl.semaphore_signal(stage_sems.at[i], inc=1, device_id=d, device_id_type=MESH)
        pl.semaphore_wait(stage_sems.at[i], len(group))


def wait_bytes(ref, sem):
    pltpu.make_async_copy(ref, ref, sem).wait()


def exchange_kernel(n_src, n_rcv, x_ref, f_ref, recv, table, f_row, stage_sems, s_x, r_x, s_f, r_f, s_g, r_g):
    S, R = lax.axis_index("src"), lax.axis_index("rcv")
    enter(S, R, n_src, n_rcv, stage_sems)

    def send_filter(j, c):
        pltpu.make_async_remote_copy(
            f_ref, f_row.at[R], s_f, r_f, device_id=(S, lax.rem(R + j, n_rcv)), device_id_type=MESH
        ).start()
        return c

    lax.fori_loop(1, n_rcv, send_filter, 0)

    def send_traces(i, c):
        dS = lax.rem(S + i // n_rcv, n_src)
        dR = lax.rem(R + lax.rem(i, n_rcv), n_rcv)
        pltpu.make_async_remote_copy(
            x_ref.at[dS, dR], recv.at[S, R], s_x, r_x.at[i // n_rcv], device_id=(dS, dR), device_id_type=MESH
        ).start()
        return c

    lax.fori_loop(1, n_src * n_rcv, send_traces, 0)
    f_row[R] = f_ref[...]
    wait_bytes(f_row.at[pl.ds(0, n_rcv - 1)], r_f)
    table[S] = f_row[...].astype(jnp.bfloat16).reshape(table.shape[1:])

    def send_rows(k, c):
        pltpu.make_async_remote_copy(
            table.at[S], table.at[S], s_g, r_g, device_id=(lax.rem(S + k, n_src), R), device_id_type=MESH
        ).start()
        return c

    lax.fori_loop(1, n_src, send_rows, 0)
    recv[S, R] = x_ref[S, R]
    wait_bytes(table.at[pl.ds(0, n_src - 1)], r_g)
    for k in range(n_src):
        wait_bytes(recv.at[0, pl.ds(0, n_rcv - (k == 0))], r_x.at[k])
    wait_bytes(f_row.at[pl.ds(0, n_rcv - 1)], s_f)
    wait_bytes(table.at[pl.ds(0, n_src - 1)], s_g)
    for k in range(n_src):
        wait_bytes(recv.at[0, pl.ds(0, n_rcv - (k == 0))], s_x)


def exchange(tiles, own_filter):
    n_src, n_rcv = tiles.shape[:2]
    vm = pl.BlockSpec(memory_space=pltpu.VMEM)
    D = pltpu.SemaphoreType.DMA
    return pl.pallas_call(
        functools.partial(exchange_kernel, n_src, n_rcv),
        out_shape=(
            jax.ShapeDtypeStruct(tiles.shape, tiles.dtype),
            jax.ShapeDtypeStruct((n_src, n_rcv * 8, 128), jnp.bfloat16),
        ),
        in_specs=[vm, vm],
        out_specs=(vm, vm),
        scratch_shapes=[
            pltpu.VMEM((n_rcv, 8, 128), jnp.float32),
            pltpu.SemaphoreType.REGULAR((3,)),
            D, D((n_src,)), D, D, D, D,
        ],
        compiler_params=pltpu.CompilerParams(
            collective_id=0, has_side_effects=True, vmem_limit_bytes=32 << 20
        ),
    )(tiles, own_filter)


def reduce_kernel(n_src, n_rcv, g_ref, o_rcv, o_src, parts, mine, s_p, r_p, s_a, r_a, s_b, r_b):
    S, R = lax.axis_index("src"), lax.axis_index("rcv")
    bar = pltpu.get_barrier_semaphore()
    for k in range(1, n_src):
        pl.semaphore_signal(bar, inc=1, device_id=(lax.rem(S + k, n_src), R), device_id_type=MESH)
    for k in range(1, n_rcv):
        pl.semaphore_signal(bar, inc=1, device_id=(S, lax.rem(R + k, n_rcv)), device_id_type=MESH)
    pl.semaphore_wait(bar, n_src + n_rcv - 2)

    def send_part(k, c):
        d = lax.rem(S + k, n_src)
        pltpu.make_async_remote_copy(
            g_ref.at[d], parts.at[S], s_p, r_p, device_id=(d, R), device_id_type=MESH
        ).start()
        return c

    lax.fori_loop(1, n_src, send_part, 0)
    parts[S] = g_ref[S]
    wait_bytes(parts.at[pl.ds(0, n_src - 1)], r_p)
    total = jnp.sum(parts[...], axis=0)
    mine[0] = total[:4]
    mine[1] = total[4:]
    o_rcv[S] = total[:4]
    o_src[R] = total[4:]

    def send_rcv(k, c):
        pltpu.make_async_remote_copy(
            mine.at[1], o_src.at[R], s_b, r_b, device_id=(S, lax.rem(R + k, n_rcv)), device_id_type=MESH
        ).start()
        return c

    lax.fori_loop(1, n_rcv, send_rcv, 0)

    def send_src(k, c):
        pltpu.make_async_remote_copy(
            mine.at[0], o_rcv.at[S], s_a, r_a, device_id=(lax.rem(S + k, n_src), R), device_id_type=MESH
        ).start()
        return c

    lax.fori_loop(1, n_src, send_src, 0)
    wait_bytes(o_rcv.at[pl.ds(0, n_src - 1)], r_a)
    wait_bytes(o_src.at[pl.ds(0, n_rcv - 1)], r_b)
    wait_bytes(parts.at[pl.ds(0, n_src - 1)], s_p)
    wait_bytes(o_rcv.at[pl.ds(0, n_src - 1)], s_a)
    wait_bytes(o_src.at[pl.ds(0, n_rcv - 1)], s_b)


def reduce_both(parts, n_rcv):
    n_src = parts.shape[0]
    vm = pl.BlockSpec(memory_space=pltpu.VMEM)
    D = pltpu.SemaphoreType.DMA
    return pl.pallas_call(
        functools.partial(reduce_kernel, n_src, n_rcv),
        out_shape=(
            jax.ShapeDtypeStruct((n_src, 4, 128), jnp.float32),
            jax.ShapeDtypeStruct((n_rcv, 4, 128), jnp.float32),
        ),
        in_specs=[vm],
        out_specs=(vm, vm),
        scratch_shapes=[
            pltpu.VMEM((n_src, 8, 128), jnp.float32),
            pltpu.VMEM((2, 4, 128), jnp.float32),
            D, D, D, D, D, D,
        ],
        compiler_params=pltpu.CompilerParams(collective_id=1, has_side_effects=True),
    )(parts)


def toeplitz_tables(tap_rows, trace_len):
    group_count, tap_count = tap_rows.shape
    period = trace_len + tap_count
    padded = jnp.concatenate(
        [tap_rows, jnp.zeros((group_count, period - tap_count), tap_rows.dtype)], axis=1
    )
    tiled = jnp.tile(padded, (1, trace_len))[:, : trace_len * (period - 1)]
    return tiled.reshape(group_count, trace_len, period - 1)[:, :, :trace_len]


def convolve(lead_traces, tap_rows):
    lead_count, row_count, trace_len = lead_traces.shape
    group_total = lead_count // station_group

    def filter_group(inputs_pair):
        trace_block, block_taps = inputs_pair
        tables = toeplitz_tables(block_taps, trace_len)
        return jnp.einsum(
            "gpu,gut->gpt", trace_block, tables, preferred_element_type=jnp.float32
        ).astype(jnp.bfloat16)

    grouped = lead_traces.reshape(group_total, station_group, row_count, trace_len)
    grouped_taps = tap_rows.reshape(group_total, station_group, tap_rows.shape[1])
    return lax.map(filter_group, (grouped, grouped_taps)).reshape(lead_count, row_count, trace_len)


def correlate(lead_residual, lead_traces, tap_count):
    lead_count, row_count, trace_len = lead_traces.shape
    group_total = lead_count // station_group
    block_len = min(128, trace_len)

    def lag_group(inputs_pair):
        residual_block, trace_block = inputs_pair
        delayed = jnp.pad(trace_block, ((0, 0), (0, 0), (tap_count, 0)))
        accumulated = jnp.zeros((station_group, tap_count), jnp.float32)
        for begin_at in range(0, trace_len, block_len):
            products = jnp.einsum(
                "gpa,gpj->gaj",
                residual_block[:, :, begin_at : begin_at + block_len],
                delayed[:, :, begin_at : begin_at + block_len + tap_count],
                preferred_element_type=jnp.float32,
            )
            flattened = products.reshape(station_group, block_len * (block_len + tap_count))
            flattened = jnp.concatenate(
                [flattened, jnp.zeros((station_group, block_len), jnp.float32)], axis=1
            )
            skewed = flattened.reshape(station_group, block_len, block_len + tap_count + 1)
            accumulated = accumulated + jnp.sum(skewed[:, :, 1 : tap_count + 1], axis=1)
        return accumulated[:, ::-1]

    grouped_residual = lead_residual.reshape(group_total, station_group, row_count, trace_len)
    grouped_traces = lead_traces.reshape(group_total, station_group, row_count, trace_len)
    return lax.map(lag_group, (grouped_residual, grouped_traces)).reshape(lead_count, tap_count)


def shards(traces, dead_mask, filters, station_of_slot):
    src_rows, rcv_cols, trace_len = traces.shape
    tap_count = filters.shape[1]
    src_count = lax.axis_size("src")
    rcv_count = lax.axis_size("rcv")
    fine_size = src_rows // rcv_count
    tiles = traces.reshape(rcv_count, 2, src_count, 2, 4, 128).transpose(2, 0, 3, 1, 4, 5)
    tiles = tiles.reshape(src_count, rcv_count, 16, 128)
    own_filter = jnp.pad(filters.astype(jnp.float32).reshape(4, 128), ((0, 4), (0, 0)))
    moved, table = exchange(tiles, own_filter)
    filter_table = table.reshape(src_count * rcv_count, 8, 128)[:, :4].reshape(-1, tap_count)
    local_rows = jnp.arange(src_rows, dtype=jnp.int32)
    local_cols = jnp.arange(rcv_cols, dtype=jnp.int32)
    row_slots = lax.axis_index("src") * src_rows + local_rows
    col_slots = (
        local_cols // fine_size * rcv_count + lax.axis_index("rcv")
    ) * fine_size + local_cols % fine_size
    row_taps = filter_table[station_of_slot[row_slots]]
    col_taps = filter_table[station_of_slot[col_slots]]
    mirrored = moved.reshape(src_count, rcv_count, 2, 2, 4, 128).transpose(1, 2, 0, 3, 4, 5)
    mirrored = mirrored.reshape(src_rows, rcv_cols, trace_len)
    by_column = jnp.transpose(traces, (1, 0, 2))
    column_filtered = convolve(by_column, col_taps)
    row_filtered = convolve(mirrored, row_taps)
    live = dead_mask.astype(jnp.float32)[:, :, None]
    residual = (
        live
        * (
            jnp.transpose(column_filtered, (1, 0, 2)).astype(jnp.float32)
            - row_filtered.astype(jnp.float32)
        )
    ).astype(jnp.bfloat16)
    scale = 1.0 / math.sqrt(src_rows * src_count * trace_len)
    receiver_terms = correlate(jnp.transpose(residual, (1, 0, 2)), by_column, tap_count) * scale
    source_terms = correlate(residual, mirrored, tap_count) * -scale
    grad_receiver = receiver_terms.reshape(src_count, 4, 128)
    sums_rcv, _ = reduce_both(jnp.concatenate([grad_receiver, grad_receiver], axis=1), rcv_count)
    grad_receiver = sums_rcv.reshape(rcv_cols, tap_count)
    grad_source = lax.psum(source_terms.astype(jnp.bfloat16), "rcv").astype(jnp.float32)
    return (residual, grad_receiver, grad_source)


def solution(mesh):
    placed = (P("src", "rcv", None), P("src", "rcv"), P(("src", "rcv"), None), P())
    return jax.shard_map(
        shards,
        mesh=mesh,
        in_specs=placed,
        out_specs=(P("src", "rcv", None), P("rcv", None), P("src", None)),
        check_vma=False,
    )
```

```python
import functools
import math

import jax
import jax.numpy as jnp
from jax import lax
from jax.experimental import pallas as pl
from jax.experimental.pallas import tpu as pltpu
from jax.sharding import PartitionSpec as P

MESH = pl.DeviceIdType.MESH
F32 = jnp.float32
BF16 = jnp.bfloat16
NB = 4
L = 128


def digits_of(n_src, n_rcv):
    if (n_src, n_rcv) == (16, 16):
        return (2, 4, 2), (4, 4)
    return (1, n_src // 2, 2), (n_rcv // 2, 2)


def line_peers(S, R, n_src, n_rcv):
    (nl, ny, nc), (nx, nh) = digits_of(n_src, n_rcv)
    l, y, c = S // (ny * nc), lax.rem(S // nc, ny), lax.rem(S, nc)
    x, h = R // nh, lax.rem(R, nh)

    def at(dl, dy, dc, dx, dh):
        s = (lax.rem(l + dl, nl) * ny + lax.rem(y + dy, ny)) * nc + lax.rem(c + dc, nc)
        return s, lax.rem(x + dx, nx) * nh + lax.rem(h + dh, nh)

    z = [at(a, 0, 0, 0, b) for a in range(nl) for b in range(nh) if a or b]
    xs = [at(0, 0, 0, a, 0) for a in range(1, nx)]
    ys = [at(0, a, 0, 0, 0) for a in range(1, ny)]
    cs = [at(0, 0, a, 0, 0) for a in range(1, nc)]
    return z, xs, ys, cs


def wait_bytes(ref, sem):
    pltpu.make_async_copy(ref, ref, sem).wait()


def iota(shape, axis):
    return lax.broadcasted_iota(jnp.int32, shape, axis)


def swap_middle(v, rows):
    place = lax.rem(iota((rows, L), 0), 16) // 4
    down = pltpu.roll(v, 4, 0)
    up = pltpu.roll(v, rows - 4, 0)
    return jnp.where(place == 1, up, jnp.where(place == 2, down, v))


def kernel(
    n_src, n_rcv, scale,
    traces, mask, filters, slots,
    residual, grad_rcv, grad_src,
    xin, xt, x3, x3t, floc, send, recv, res,
    m128, mt, fm, f_row, table, tabf, ctaps, g128, gsnd, hrec, pown, prec, toep,
    gmsg, parts, mine,
    stage_sems, s_in, s_x, r_x, s_f, r_f, s_g, r_g, s_h, r_h, s_p, r_p, s_a, r_a, s_b, r_b,
):
    S, R = lax.axis_index("src"), lax.axis_index("rcv")
    rows_p, cols_q = 2 * n_rcv, 2 * n_src
    rows = n_rcv * 16

    z, xs, ys, cs = line_peers(S, R, n_src, n_rcv)
    bar = pltpu.get_barrier_semaphore()
    near = z + xs + ys + cs
    for d in near:
        pl.semaphore_signal(bar, inc=1, device_id=d, device_id_type=MESH)
    load = pltpu.make_async_copy(traces, xin, s_in)
    load.start()

    m128[...] = jnp.zeros((L, L), F32)
    m128[0:rows_p, 0:cols_q] = mask[...].astype(F32)
    mt[...] = jnp.transpose(m128[...])
    f = filters[...].astype(F32)
    fm[...] = jnp.zeros(fm.shape, F32)
    for r in range(n_rcv):
        fm[r, 0:2, :] = f[:, :L]
        fm[r, 2:4, :] = f[:, L:]
        fm[r, 4:6, :] = m128[2 * r : 2 * r + 2, :]

    pl.semaphore_wait(bar, len(near))
    for i, group in enumerate((xs, ys, cs)):
        for d in group:
            pl.semaphore_signal(stage_sems.at[i], inc=1, device_id=d, device_id_type=MESH)
        pl.semaphore_wait(stage_sems.at[i], len(group))

    own8 = pl.ds(pl.multiple_of(R * 8, 8), 8)

    def send_filter(j, c):
        d = lax.rem(R + j, n_rcv)
        pltpu.make_async_remote_copy(
            fm.at[d], f_row.at[own8], s_f, r_f, device_id=(S, d), device_id_type=MESH
        ).start()
        return c

    lax.fori_loop(1, n_rcv, send_filter, 0)
    f_row[own8, :] = fm[R]

    load.wait()

    def spread(p, c):
        for b in range(NB):
            xt[p, pl.ds(b, cols_q, stride=NB), :] = xin[p, :, b * L : (b + 1) * L].astype(F32)
        return c

    lax.fori_loop(0, rows_p, spread, 0)
    row = iota((rows, L), 0)
    lane = iota((rows, L), 1)
    block = lax.rem(row, NB)
    q2 = lax.rem(row // NB, 2)
    p2 = lax.rem(row // (2 * NB), 2)
    tile = row // 16
    pown[...] = jnp.where(lane == 2 * tile + p2, 1.0, 0.0)
    prec[...] = jnp.where(lane == 64 + q2 * n_rcv + tile, 1.0, 0.0)
    flip = jnp.where(iota((L, L), 0) + iota((L, L), 1) == L - 1, 1.0, 0.0).astype(BF16)

    def delays(s, c):
        x = xt[:, pl.ds(pl.multiple_of(s * 8, 8), 8), :].reshape(rows, L)
        for d in range(3):
            v = x if d == 0 else jnp.where(block >= d, pltpu.roll(x, d, 0), 0.0)
            v = v.astype(BF16)
            at = (2 - d) * L
            x3[s, :, at : at + L] = v
            x3t[s, at : at + L, :] = lax.dot_general(
                flip, v, (((1,), (1,)), ((), ())), preferred_element_type=F32
            ).astype(BF16)
        return c

    lax.fori_loop(0, n_src, delays, 0)

    wait_bytes(f_row.at[pl.ds(0, (n_rcv - 1) * 8)], r_f)
    for i in range(4):
        table[S, i * n_rcv : (i + 1) * n_rcv, :] = f_row[pl.ds(i, n_rcv, stride=8), :].astype(BF16)
    g128[...] = jnp.zeros((L, L), F32)
    for i in range(2):
        g128[64 + i * n_rcv : 64 + (i + 1) * n_rcv, :] = f_row[pl.ds(4 + i, n_rcv, stride=8), :]
    gt = jnp.transpose(g128[...])
    gsnd[...] = jnp.zeros(gsnd.shape, F32)
    for s in range(n_src):
        gsnd[s, 0:2, :] = gt[2 * s : 2 * s + 2, :]

    def send_rows(k, c):
        d = lax.rem(S + k, n_src)
        pltpu.make_async_remote_copy(
            table.at[S], table.at[S], s_g, r_g, device_id=(d, R), device_id_type=MESH
        ).start()
        pltpu.make_async_remote_copy(
            gsnd.at[d], hrec.at[S], s_h, r_h, device_id=(d, R), device_id_type=MESH
        ).start()
        return c

    lax.fori_loop(1, n_src, send_rows, 0)
    hrec[S] = gsnd[S]
    wait_bytes(table.at[pl.ds(0, n_src - 1)], r_g)
    tabf[...] = table[...].astype(F32).reshape(tabf.shape)

    def pick(w, c):
        slot = ((w // 2) * n_rcv + R) * 2 + lax.rem(w, 2)
        st = slots[slot]
        at = (st // (2 * n_rcv)) * (4 * n_rcv) + lax.rem(st, 2) * n_rcv + lax.rem(st // 2, n_rcv)
        ctaps[pl.ds(w, 1), :] = tabf[pl.ds(at, 1), :]
        ctaps[pl.ds(cols_q + w, 1), :] = tabf[pl.ds(at + 2 * n_rcv, 1), :]
        return c

    lax.fori_loop(0, cols_q, pick, 0)

    later = iota((L, L), 1) >= iota((L, L), 0)

    def filter_pair(k, first):
        s = lax.rem(S + k, n_src)
        for i in range(2):
            q = 2 * s + i
            c0 = jnp.broadcast_to(ctaps[pl.ds(q, 1), :], (L, L))
            c1 = jnp.broadcast_to(ctaps[pl.ds(cols_q + q, 1), :], (L, L))
            c0 = pltpu.roll(c0, 0, 1, stride=1, stride_axis=0)
            c1 = pltpu.roll(c1, 0, 1, stride=1, stride_axis=0)
            at = slice(i * L, (i + 1) * L)
            toep[0:L, at] = jnp.where(later, 0.0, c1).astype(BF16)
            toep[L : 2 * L, at] = jnp.where(later, c1, c0).astype(BF16)
            toep[2 * L : 3 * L, at] = jnp.where(later, c0, 0.0).astype(BF16)
        y = jnp.dot(x3[s], toep[...], preferred_element_type=F32)
        y = jnp.where(q2 == 1, y[:, L:], y[:, :L]).astype(BF16)
        floc[s] = y
        send[s] = swap_middle(y.astype(F32), rows).astype(BF16).reshape(n_rcv, 16, L)
        for j in range(1 if first else 0, n_rcv):
            d = lax.rem(R + j, n_rcv)
            pltpu.make_async_remote_copy(
                send.at[s, d], recv.at[S, R], s_x, r_x.at[k], device_id=(s, d), device_id_type=MESH
            ).start()

    filter_pair(0, True)
    recv[S, R] = send[S, R]

    def filter_step(k, c):
        filter_pair(k, False)
        return c

    lax.fori_loop(1, n_src, filter_step, 0)
    wait_bytes(hrec.at[pl.ds(0, n_src - 1)], r_h)

    reach = iota((L, L), 1) + iota((L, L), 0) >= L - 1
    spread_ones = jnp.where((iota((L, 2 * L), 0) < 64) == (iota((L, 2 * L), 1) < L), 1.0, 0.0).astype(BF16)

    def lag_pair(k, first):
        s = lax.rem(S + n_src - k, n_src)
        wait_bytes(recv.at[0, pl.ds(0, n_rcv - (1 if first else 0))], r_x.at[k])
        diff = floc[s].astype(F32) - recv[s].reshape(rows, L).astype(F32)
        own = jnp.where(q2 == 0, mt[pl.ds(2 * s, 1), :], mt[pl.ds(2 * s + 1, 1), :])
        other = jnp.where(p2 == 0, hrec[s, 0:1, :], hrec[s, 1:2, :])
        live = pown[...] * own + prec[...] * other
        live = jnp.dot(live.astype(BF16), spread_ones, preferred_element_type=F32)
        found = []
        for t in range(2):
            r = live[:, t * L : (t + 1) * L] * diff
            if t == 0:
                res[:, pl.ds(pl.multiple_of(s * 8, 8), 8), :] = r.reshape(rows_p, 8, L)
            both = jnp.concatenate([jnp.where(q2 == 0, r, 0.0), jnp.where(q2 == 1, r, 0.0)], axis=1)
            m = jnp.dot(x3t[s], both.astype(BF16), preferred_element_type=F32)
            for i in range(2):
                mi = m[:, i * L : (i + 1) * L]
                m2, m1, m0 = mi[0:L], mi[L : 2 * L], mi[2 * L : 3 * L]
                for a, b in ((m0, m1), (m1, m2)):
                    skew = pltpu.roll(jnp.where(reach, a, b), 1, 1, stride=1, stride_axis=0)
                    found.append(jnp.sum(skew, axis=0, keepdims=True))
        msg = jnp.concatenate(found, axis=0)
        if first:
            parts[S] = msg
        else:
            gmsg[s] = msg
            pltpu.make_async_remote_copy(
                gmsg.at[s], parts.at[S], s_p, r_p, device_id=(s, R), device_id_type=MESH
            ).start()

    lag_pair(0, True)

    def lag_step(k, c):
        lag_pair(k, False)
        return c

    lax.fori_loop(1, n_src, lag_step, 0)

    def gather(p, c):
        for b in range(NB):
            residual[p, :, b * L : (b + 1) * L] = res[p, pl.ds(b, cols_q, stride=NB), :].astype(BF16)
        return c

    lax.fori_loop(0, rows_p, gather, 0)

    wait_bytes(parts.at[pl.ds(0, n_src - 1)], r_p)
    total = jnp.sum(parts[...], axis=0) * scale
    mine[0] = total[:4]
    mine[1] = total[4:]
    grad_rcv[S] = total[:4]
    grad_src[R] = total[4:]

    def send_rcv(k, c):
        pltpu.make_async_remote_copy(
            mine.at[1], grad_src.at[R], s_b, r_b, device_id=(S, lax.rem(R + k, n_rcv)), device_id_type=MESH
        ).start()
        return c

    lax.fori_loop(1, n_rcv, send_rcv, 0)

    def send_src(k, c):
        pltpu.make_async_remote_copy(
            mine.at[0], grad_rcv.at[S], s_a, r_a, device_id=(lax.rem(S + k, n_src), R), device_id_type=MESH
        ).start()
        return c

    lax.fori_loop(1, n_src, send_src, 0)
    wait_bytes(f_row.at[pl.ds(0, (n_rcv - 1) * 8)], s_f)
    wait_bytes(table.at[pl.ds(0, n_src - 1)], s_g)
    wait_bytes(hrec.at[pl.ds(0, n_src - 1)], s_h)
    wait_bytes(parts.at[pl.ds(0, n_src - 1)], s_p)
    for k in range(n_src):
        wait_bytes(recv.at[0, pl.ds(0, n_rcv - (k == 0))], s_x)
    wait_bytes(grad_rcv.at[pl.ds(0, n_src - 1)], r_a)
    wait_bytes(grad_src.at[pl.ds(0, n_rcv - 1)], r_b)
    wait_bytes(grad_rcv.at[pl.ds(0, n_src - 1)], s_a)
    wait_bytes(grad_src.at[pl.ds(0, n_rcv - 1)], s_b)


def shards(traces, dead_mask, filters, station_of_slot):
    rows_p, cols_q, trace_len = traces.shape
    tap_count = filters.shape[1]
    n_src, n_rcv = lax.axis_size("src"), lax.axis_size("rcv")
    rows = n_rcv * 16
    scale = 1.0 / math.sqrt(rows_p * n_src * trace_len)
    vm = pl.BlockSpec(memory_space=pltpu.VMEM)
    V = pltpu.VMEM
    D = pltpu.SemaphoreType.DMA
    residual, grad_rcv, grad_src = pl.pallas_call(
        functools.partial(kernel, n_src, n_rcv, scale),
        out_shape=(
            jax.ShapeDtypeStruct(traces.shape, BF16),
            jax.ShapeDtypeStruct((n_src, 4, L), F32),
            jax.ShapeDtypeStruct((n_rcv, 4, L), F32),
        ),
        in_specs=[pl.BlockSpec(memory_space=pl.ANY), vm, vm, pl.BlockSpec(memory_space=pltpu.SMEM)],
        out_specs=(vm, vm, vm),
        scratch_shapes=[
            V(traces.shape, BF16),
            V((rows_p, NB * cols_q, L), F32),
            V((n_src, rows, 3 * L), BF16),
            V((n_src, 3 * L, rows), BF16),
            V((n_src, rows, L), BF16),
            V((n_src, n_rcv, 16, L), BF16),
            V((n_src, n_rcv, 16, L), BF16),
            V((rows_p, NB * cols_q, L), F32),
            V((L, L), F32),
            V((L, L), F32),
            V((n_rcv, 8, L), F32),
            V((n_rcv * 8, L), F32),
            V((n_src, 4 * n_rcv, L), BF16),
            V((n_src * 4 * n_rcv, L), F32),
            V((2 * cols_q, L), F32),
            V((L, L), F32),
            V((n_src, 8, L), F32),
            V((n_src, 8, L), F32),
            V((rows, L), F32),
            V((rows, L), F32),
            V((3 * L, 2 * L), BF16),
            V((n_src, 8, L), F32),
            V((n_src, 8, L), F32),
            V((2, 4, L), F32),
            pltpu.SemaphoreType.REGULAR((3,)),
            D, D, D((n_src,)), D, D, D, D, D, D, D, D, D, D, D, D,
        ],
        compiler_params=pltpu.CompilerParams(
            collective_id=0, has_side_effects=True, vmem_limit_bytes=48 << 20
        ),
    )(traces, dead_mask, filters, station_of_slot)
    return residual, grad_rcv.reshape(cols_q, tap_count), grad_src.reshape(rows_p, tap_count)


def solution(mesh):
    placed = (P("src", "rcv", None), P("src", "rcv"), P(("src", "rcv"), None), P())
    return jax.shard_map(
        shards,
        mesh=mesh,
        in_specs=placed,
        out_specs=(P("src", "rcv", None), P("rcv", None), P("src", None)),
        check_vma=False,
    )
```

```python
import functools
import math

import jax
import jax.numpy as jnp
from jax import lax
from jax.experimental import pallas as pl
from jax.experimental.pallas import tpu as pltpu
from jax.sharding import PartitionSpec as P

MESH = pl.DeviceIdType.MESH
F32 = jnp.float32
BF16 = jnp.bfloat16
NB = 4
L = 128
RAW = 4


def digits_of(n_src, n_rcv):
    if (n_src, n_rcv) == (16, 16):
        return (2, 4, 2), (4, 4)
    return (1, n_src // 2, 2), (n_rcv // 2, 2)


def rcv_offsets(nx, nh):
    def far(d):
        return 2 * min(d[1], nh - d[1]), min(d[0], nx - d[0])

    return sorted([(a, b) for a in range(nx) for b in range(nh)], key=far, reverse=True)


def raw_of(n_rcv):
    return n_rcv * RAW // 16


def wait_bytes(ref, sem):
    pltpu.make_async_copy(ref, ref, sem).wait()


def iota(shape, axis):
    return lax.broadcasted_iota(jnp.int32, shape, axis)


def swap_middle(a, b):
    low = iota(a.shape, 1) < 4
    ra, rb = pltpu.roll(a, 4, 1), pltpu.roll(b, 4, 1)
    w0, w1 = jnp.where(low, a, rb), jnp.where(low, ra, b)
    return jnp.concatenate([w0, w1], axis=1).astype(BF16)


def delayed(x):
    block = lax.rem(iota(x.shape, 1), NB)
    n = x.shape[0] * 8
    out = [x]
    for d in (1, 2):
        out.append(jnp.where(block >= d, pltpu.roll(x, d, 1), 0.0))
    return [v.reshape(n, L).astype(BF16) for v in out]


def toeplitz(c0, c1, later, out, at):
    c0 = pltpu.roll(jnp.broadcast_to(c0, (L, L)), 0, 1, stride=1, stride_axis=0)
    c1 = pltpu.roll(jnp.broadcast_to(c1, (L, L)), 0, 1, stride=1, stride_axis=0)
    out[0:L, at : at + L] = jnp.where(later, 0.0, c1).astype(BF16)
    out[L : 2 * L, at : at + L] = jnp.where(later, c1, c0).astype(BF16)
    out[2 * L : 3 * L, at : at + L] = jnp.where(later, c0, 0.0).astype(BF16)


def kernel(
    n_src, n_rcv, scale,
    traces, mask, filters, slots,
    residual, grad_rcv, grad_src,
    xin, mask_in, filt_in, slots_in,
    xt, x3, x3t, floc, send, raw, recv, res, live,
    m128, mt, fm, f_row, table, tabf, taps, g128, gsnd, hrec, toep, x3m,
    gmsg, parts, mine, land_r, land_s, order_r, order_s,
    stage_sems, s_in, s_x, r_x, s_w, r_w, s_f, r_f, s_g, r_g, s_h, r_h, s_p, r_p, s_a, r_a, s_b, r_b,
):
    S, R = lax.axis_index("src"), lax.axis_index("rcv")
    rows_p, cols_q = 2 * n_rcv, 2 * n_src
    rows = n_rcv * 16
    (nl, ny, nc), (nx, nh) = digits_of(n_src, n_rcv)
    l, y, c = S // (ny * nc), lax.rem(S // nc, ny), lax.rem(S, nc)
    x, h = R // nh, lax.rem(R, nh)

    def at_src(dl, dy, dc):
        return (lax.rem(l + dl, nl) * ny + lax.rem(y + dy, ny)) * nc + lax.rem(c + dc, nc)

    def at_rcv(dx, dh):
        return lax.rem(x + dx, nx) * nh + lax.rem(h + dh, nh)

    z = [(at_src(a, 0, 0), at_rcv(0, b)) for a in range(nl) for b in range(nh) if a or b]
    xs = [(S, at_rcv(a, 0)) for a in range(1, nx)]
    ys = [(at_src(0, a, 0), R) for a in range(1, ny)]
    cs = [(at_src(0, 0, a), R) for a in range(1, nc)]
    bar = pltpu.get_barrier_semaphore()
    near = z + xs + ys + cs
    for d in near:
        pl.semaphore_signal(bar, inc=1, device_id=d, device_id_type=MESH)
    loads = [
        pltpu.make_async_copy(a, b, s_in.at[i])
        for i, (a, b) in enumerate(
            ((filters, filt_in), (mask, mask_in), (slots, slots_in), (traces, xin))
        )
    ]
    for a in loads:
        a.start()

    def stage(i, group):
        for d in group:
            pl.semaphore_signal(stage_sems.at[i], inc=1, device_id=d, device_id_type=MESH)

    offsets = rcv_offsets(nx, nh)
    n_raw = raw_of(n_rcv)
    to_rcv = [at_rcv(a, b) for a, b in offsets]
    from_rcv = [at_rcv(nx - a, nh - b) for a, b in offsets[:n_raw]]

    m128[...] = jnp.zeros((L, L), F32)
    fm[...] = jnp.zeros(fm.shape, F32)
    g128[...] = jnp.zeros((L, L), F32)
    gsnd[...] = jnp.zeros(gsnd.shape, F32)
    loads[0].wait()
    f = filt_in[...].astype(F32)
    loads[1].wait()
    m128[0:rows_p, 0:cols_q] = mask_in[...].astype(F32)
    for r in range(n_rcv):
        fm[r, 0:2, :] = f[:, :L]
        fm[r, 2:4, :] = f[:, L:]
        fm[r, 4:6, :] = m128[2 * r : 2 * r + 2, :]

    pl.semaphore_wait(bar, len(near))
    stage(0, xs)
    loads[2].wait()
    loads[3].wait()

    def spread(p, carry):
        for b in range(NB):
            xt[p, pl.ds(b, cols_q, stride=NB), :] = xin[p, :, b * L : (b + 1) * L].astype(F32)
        return carry

    lax.fori_loop(0, rows_p, spread, 0)
    pl.semaphore_wait(stage_sems.at[0], len(xs))

    own8 = pl.ds(pl.multiple_of(R * 8, 8), 8)
    for d in to_rcv[:-1]:
        pltpu.make_async_remote_copy(
            fm.at[d], f_row.at[own8], s_f, r_f, device_id=(S, d), device_id_type=MESH
        ).start()
    stage(1, ys)
    f_row[own8, :] = fm[R]
    for i, d in enumerate(to_rcv[:n_raw]):
        a = xt[2 * d].reshape(n_src, 8, L)
        b = xt[2 * d + 1].reshape(n_src, 8, L)
        raw[i] = swap_middle(a, b)
    mt[...] = jnp.transpose(m128[...])
    pl.semaphore_wait(stage_sems.at[1], len(ys))
    stage(2, cs)
    pl.semaphore_wait(stage_sems.at[2], len(cs))

    for i, d in enumerate(to_rcv[:n_raw]):
        def send_raw(k, carry):
            s = lax.rem(S + k, n_src)
            pltpu.make_async_remote_copy(
                raw.at[i, s], recv.at[S, R], s_w, r_w.at[i], device_id=(s, d), device_id_type=MESH
            ).start()
            return carry

        lax.fori_loop(0, n_src, send_raw, 0)

    wait_bytes(f_row.at[pl.ds(0, (n_rcv - 1) * 8)], r_f)
    for i in range(4):
        table[S, i * n_rcv : (i + 1) * n_rcv, :] = f_row[pl.ds(i, n_rcv, stride=8), :].astype(BF16)

    def send_table(k, carry):
        pltpu.make_async_remote_copy(
            table.at[S], table.at[S], s_g, r_g, device_id=(lax.rem(S + k, n_src), R), device_id_type=MESH
        ).start()
        return carry

    lax.fori_loop(1, n_src, send_table, 0)
    for i in range(2):
        g128[64 + i * n_rcv : 64 + (i + 1) * n_rcv, :] = f_row[pl.ds(4 + i, n_rcv, stride=8), :]
    gt = jnp.transpose(g128[...])
    for s in range(n_src):
        gsnd[s, 0:2, :] = gt[2 * s : 2 * s + 2, :]

    def send_live(k, carry):
        d = lax.rem(S + k, n_src)
        pltpu.make_async_remote_copy(
            gsnd.at[d], hrec.at[S], s_h, r_h, device_id=(d, R), device_id_type=MESH
        ).start()
        return carry

    lax.fori_loop(1, n_src, send_live, 0)
    hrec[S] = gsnd[S]
    flip = jnp.where(iota((L, L), 0) + iota((L, L), 1) == L - 1, 1.0, 0.0).astype(BF16)

    def delays(s, carry):
        v3 = delayed(xt[:, pl.ds(pl.multiple_of(s * 8, 8), 8), :])
        for d in range(3):
            at = (2 - d) * L
            x3[s, :, at : at + L] = v3[d]
            x3t[s, at : at + L, :] = lax.dot_general(
                flip, v3[d], (((1,), (1,)), ((), ())), preferred_element_type=F32
            ).astype(BF16)
        return carry

    lax.fori_loop(0, n_src, delays, 0)

    wait_bytes(table.at[pl.ds(0, n_src - 1)], r_g)
    tabf[...] = table[...].astype(F32).reshape(tabf.shape)

    def pick(slot, w):
        st = slots_in[slot]
        at = (st // (2 * n_rcv)) * (4 * n_rcv) + lax.rem(st, 2) * n_rcv + lax.rem(st // 2, n_rcv)
        taps[pl.ds(2 * w, 1), :] = tabf[pl.ds(at, 1), :]
        taps[pl.ds(2 * w + 1, 1), :] = tabf[pl.ds(at + 2 * n_rcv, 1), :]

    def pick_pair(w, carry):
        slot = (w * n_rcv + R) * 2
        pick(slot, 2 * w)
        pick(slot + 1, 2 * w + 1)
        return carry

    lax.fori_loop(0, n_src, pick_pair, 0)
    for i, d in enumerate(from_rcv):
        for p in range(2):
            pick(S * rows_p + 2 * d + p, cols_q + 2 * i + p)

    later = iota((L, L), 1) >= iota((L, L), 0)
    row8 = iota((rows // 8, 8, L), 1)
    q2 = (row8 // NB).reshape(rows, L)
    p2 = lax.rem(iota((rows, L), 0) // (2 * NB), 2)

    def offset_of(i):
        o = n_src - 1 - i
        return lax.rem(o // nc, nl), o // (nc * nl), lax.rem(o, nc)

    def pair_taps(w, out):
        for i in range(2):
            at = 4 * w + 2 * i
            toeplitz(taps[pl.ds(at, 1), :], taps[pl.ds(at + 1, 1), :], later, out, i * L)

    def filter_two(i0, last):
        to = []
        for u in range(2):
            dl, dy, dc = offset_of(i0 + u)
            s = at_src(dl, dy, dc)
            to.append(s)
            pair_taps(s, toep.at[u])
        for u, s in enumerate(to):
            v = jnp.dot(x3[s], toep[u], preferred_element_type=F32)
            v = jnp.where(q2 == 1, v[:, L:], v[:, :L]).astype(BF16)
            floc[s] = v
            v = v.astype(F32).reshape(n_rcv, 2, 8, L)
            send[s] = swap_middle(v[:, 0], v[:, 1])
        for u, s in enumerate(to):
            own = last and u == 1
            for d in to_rcv[n_raw : n_rcv - (1 if own else 0)]:
                pltpu.make_async_remote_copy(
                    send.at[s, d], recv.at[S, R], s_x, r_x.at[i0 + u], device_id=(s, d), device_id_type=MESH
                ).start()

    def filter_step(i, carry):
        filter_two(2 * i, False)
        return carry

    lax.fori_loop(0, n_src // 2 - 1, filter_step, 0)
    filter_two(n_src - 2, True)
    recv[S, R] = send[S, R]

    for i, d in enumerate(from_rcv):
        wait_bytes(recv.at[0], r_w.at[i])
        v = recv[:, pl.ds(d, 1)].reshape(rows // 8, 8, L).astype(F32)
        v3 = delayed(v)
        for k in range(3):
            x3m[i % 2, :, (2 - k) * L : (3 - k) * L] = v3[k]
        pair_taps(n_src + i, toep.at[i % 2])
        v = jnp.dot(x3m[i % 2], toep[i % 2], preferred_element_type=F32)
        v = jnp.where(p2 == 1, v[:, L:], v[:, :L]).astype(BF16)
        recv[:, pl.ds(d, 1)] = v.reshape(n_src, 1, 16, L)

    wait_bytes(hrec.at[pl.ds(0, n_src - 1)], r_h)
    lane = iota((rows, L), 1)
    tile = iota((rows, L), 0) // 16
    pown = lane == 2 * tile + p2
    prec = lane == 64 + q2 * n_rcv + tile
    ones = jnp.where((iota((L, 2 * L), 0) < 64) == (iota((L, 2 * L), 1) < L), 1.0, 0.0).astype(BF16)

    def widen(i, carry):
        for u in range(2):
            s = 2 * i + u
            own = jnp.where(q2 == 0, mt[pl.ds(2 * s, 1), :], mt[pl.ds(2 * s + 1, 1), :])
            other = jnp.where(p2 == 0, hrec[s, 0:1, :], hrec[s, 1:2, :])
            v = jnp.where(pown, own, jnp.where(prec, other, 0.0)).astype(BF16)
            live[s] = jnp.dot(v, ones, preferred_element_type=F32).astype(BF16)
        return carry

    lax.fori_loop(0, n_src // 2, widen, 0)

    reach = iota((L, L), 1) + iota((L, L), 0) >= L - 1

    def lag_pairs(i0, count, last):
        found = []
        for u in range(count):
            dl, dy, dc = offset_of(i0 + u)
            s = at_src(nl - dl, ny - dy, nc - dc)
            wait_bytes(recv.at[0, pl.ds(0, n_rcv - n_raw - (1 if last else 0))], r_x.at[i0 + u])
            found.append(s)
        ms = []
        for s in found:
            diff = floc[s].astype(F32) - recv[s].reshape(rows, L).astype(F32)
            lv = live[s].astype(F32)
            for t in range(2):
                r = lv[:, t * L : (t + 1) * L] * diff
                if t == 0:
                    res[:, pl.ds(pl.multiple_of(s * 8, 8), 8), :] = r.reshape(rows_p, 8, L)
                both = jnp.concatenate([jnp.where(q2 == 0, r, 0.0), jnp.where(q2 == 1, r, 0.0)], axis=1)
                ms.append(jnp.dot(x3t[s], both.astype(BF16), preferred_element_type=F32))
        for u, s in enumerate(found):
            sums = []
            for t in range(2):
                m = ms[2 * u + t]
                for i in range(2):
                    mi = m[:, i * L : (i + 1) * L]
                    m2, m1, m0 = mi[0:L], mi[L : 2 * L], mi[2 * L : 3 * L]
                    for a, b in ((m0, m1), (m1, m2)):
                        skew = pltpu.roll(jnp.where(reach, a, b), 1, 1, stride=1, stride_axis=0)
                        sums.append(jnp.sum(skew, axis=0, keepdims=True))
            msg = jnp.concatenate(sums, axis=0)
            if last:
                parts[S] = msg
            else:
                gmsg[s] = msg
                pltpu.make_async_remote_copy(
                    gmsg.at[s], parts.at[S], s_p, r_p, device_id=(s, R), device_id_type=MESH
                ).start()

    def lag_step(i, carry):
        lag_pairs(2 * i, 2, False)
        return carry

    lax.fori_loop(0, n_src // 2 - 1, lag_step, 0)
    lag_pairs(n_src - 2, 1, False)
    lag_pairs(n_src - 1, 1, True)

    wait_bytes(parts.at[pl.ds(0, n_src - 1)], r_p)
    total = jnp.sum(parts[...], axis=0) * scale
    mine[0] = total[:4]
    mine[1] = total[4:]
    for d in to_rcv[:-1]:
        pltpu.make_async_remote_copy(
            mine.at[1], land_s.at[R], s_b, r_b, device_id=(S, d), device_id_type=MESH
        ).start()

    def send_src(k, carry):
        pltpu.make_async_remote_copy(
            mine.at[0], land_r.at[S], s_a, r_a, device_id=(lax.rem(S + k, n_src), R), device_id_type=MESH
        ).start()
        return carry

    lax.fori_loop(1, n_src, send_src, 0)
    land_r[S] = total[:4]
    land_s[R] = total[4:]

    def gather(p, carry):
        for b in range(NB):
            residual[p, :, b * L : (b + 1) * L] = res[p, pl.ds(b, cols_q, stride=NB), :].astype(BF16)
        return carry

    lax.fori_loop(0, rows_p, gather, 0)
    wait_bytes(f_row.at[pl.ds(0, (n_rcv - 1) * 8)], s_f)
    wait_bytes(table.at[pl.ds(0, n_src - 1)], s_g)
    wait_bytes(hrec.at[pl.ds(0, n_src - 1)], s_h)
    wait_bytes(parts.at[pl.ds(0, n_src - 1)], s_p)
    wait_bytes(raw, s_w)
    for i in range(n_src):
        wait_bytes(recv.at[0, pl.ds(0, n_rcv - n_raw - (1 if i == n_src - 1 else 0))], s_x)
    wait_bytes(land_r.at[pl.ds(0, n_src - 1)], s_a)
    wait_bytes(land_s.at[pl.ds(0, n_rcv - 1)], s_b)
    wait_bytes(land_r.at[pl.ds(0, n_src - 1)], r_a)
    wait_bytes(land_s.at[pl.ds(0, n_rcv - 1)], r_b)
    for i in range(2):
        for k in range(2):
            order_r[k, pl.ds(i, n_src, stride=2), :] = land_r[:, 2 * i + k, :]
            order_s[k, pl.ds(i, n_rcv, stride=2), :] = land_s[:, 2 * i + k, :]
    for k in range(2):
        at = slice(k * L, (k + 1) * L)
        grad_rcv[:, at] = order_r[k]
        grad_src[:, at] = order_s[k]


def shards(traces, dead_mask, filters, station_of_slot):
    rows_p, cols_q, trace_len = traces.shape
    tap_count = filters.shape[1]
    n_src, n_rcv = lax.axis_size("src"), lax.axis_size("rcv")
    rows = n_rcv * 16
    n_raw = raw_of(n_rcv)
    scale = 1.0 / math.sqrt(rows_p * n_src * trace_len)
    vm = pl.BlockSpec(memory_space=pltpu.VMEM)
    hbm = pl.BlockSpec(memory_space=pltpu.HBM)
    V = pltpu.VMEM
    D = pltpu.SemaphoreType.DMA
    shapes = (
        jax.ShapeDtypeStruct(traces.shape, BF16),
        jax.ShapeDtypeStruct((cols_q, tap_count), F32),
        jax.ShapeDtypeStruct((rows_p, tap_count), F32),
    )
    outs = pl.pallas_call(
        functools.partial(kernel, n_src, n_rcv, scale),
        out_shape=shapes,
        in_specs=[hbm] * 4,
        out_specs=(vm, vm, vm),
        scratch_shapes=[
            V(traces.shape, BF16),
            V(dead_mask.shape, jnp.int32),
            V(filters.shape, BF16),
            pltpu.SMEM(station_of_slot.shape, jnp.int32),
            V((rows_p, NB * cols_q, L), F32),
            V((n_src, rows, 3 * L), BF16),
            V((n_src, 3 * L, rows), BF16),
            V((n_src, rows, L), BF16),
            V((n_src, n_rcv, 16, L), BF16),
            V((n_raw, n_src, 16, L), BF16),
            V((n_src, n_rcv, 16, L), BF16),
            V((rows_p, NB * cols_q, L), F32),
            V((n_src, rows, 2 * L), BF16),
            V((L, L), F32),
            V((L, L), F32),
            V((n_rcv, 8, L), F32),
            V((n_rcv * 8, L), F32),
            V((n_src, 4 * n_rcv, L), BF16),
            V((n_src * 4 * n_rcv, L), F32),
            V((2 * cols_q + 4 * n_raw, L), F32),
            V((L, L), F32),
            V((n_src, 8, L), F32),
            V((n_src, 8, L), F32),
            V((2, 3 * L, 2 * L), BF16),
            V((2, rows, 3 * L), BF16),
            V((n_src, 8, L), F32),
            V((n_src, 8, L), F32),
            V((2, 4, L), F32),
            V((n_src, 4, L), F32),
            V((n_rcv, 4, L), F32),
            V((2, cols_q, L), F32),
            V((2, rows_p, L), F32),
            pltpu.SemaphoreType.REGULAR((3,)),
            D((4,)), D, D((n_src,)), D, D((n_raw,)),
            D, D, D, D, D, D, D, D, D, D, D, D,
        ],
        compiler_params=pltpu.CompilerParams(
            collective_id=0, has_side_effects=True, vmem_limit_bytes=60 << 20
        ),
    )(traces, dead_mask, filters, station_of_slot)
    return outs


def solution(mesh):
    placed = (P("src", "rcv", None), P("src", "rcv"), P(("src", "rcv"), None), P())
    return jax.shard_map(
        shards,
        mesh=mesh,
        in_specs=placed,
        out_specs=(P("src", "rcv", None), P("rcv", None), P("src", None)),
        check_vma=False,
    )
```

```python
import functools
import math

import jax
import jax.numpy as jnp
from jax import lax
from jax.experimental import pallas as pl
from jax.experimental.pallas import tpu as pltpu
from jax.sharding import PartitionSpec as P

MESH = pl.DeviceIdType.MESH
F32 = jnp.float32
BF16 = jnp.bfloat16
NB = 4
L = 128
RAW = 8
AHEAD = 2


def digits_of(n_src, n_rcv):
    if (n_src, n_rcv) == (16, 16):
        return (2, 4, 2), (4, 4)
    return (1, n_src // 2, 2), (n_rcv // 2, 2)


def rcv_offsets(nx, nh):
    def far(d):
        return 2 * min(d[1], nh - d[1]), min(d[0], nx - d[0])

    return sorted([(a, b) for a in range(nx) for b in range(nh)], key=far, reverse=True)


def raw_of(n_rcv):
    return n_rcv * RAW // 16


def wait_bytes(ref, sem):
    pltpu.make_async_copy(ref, ref, sem).wait()


def iota(shape, axis):
    return lax.broadcasted_iota(jnp.int32, shape, axis)


def swap_middle(a, b):
    low = iota(a.shape, 1) < 4
    ra, rb = pltpu.roll(a, 4, 1), pltpu.roll(b, 4, 1)
    w0, w1 = jnp.where(low, a, rb), jnp.where(low, ra, b)
    return jnp.concatenate([w0, w1], axis=1).astype(BF16)


def delayed(x):
    block = lax.rem(iota(x.shape, 1), NB)
    n = x.shape[0] * 8
    out = [x]
    for d in (1, 2):
        out.append(jnp.where(block >= d, pltpu.roll(x, d, 1), 0.0))
    return [v.reshape(n, L).astype(BF16) for v in out]


def toeplitz(c0, c1, later, out, at):
    c0 = pltpu.roll(jnp.broadcast_to(c0, (L, L)), 0, 1, stride=1, stride_axis=0)
    c1 = pltpu.roll(jnp.broadcast_to(c1, (L, L)), 0, 1, stride=1, stride_axis=0)
    out[0:L, at : at + L] = jnp.where(later, 0.0, c1).astype(BF16)
    out[L : 2 * L, at : at + L] = jnp.where(later, c1, c0).astype(BF16)
    out[2 * L : 3 * L, at : at + L] = jnp.where(later, c0, 0.0).astype(BF16)


def kernel(
    n_src, n_rcv, scale,
    traces, mask, filters, slots,
    residual, grad_rcv, grad_src,
    xin, mask_in, filt_in, slots_in,
    xt, x3, x3t, floc, send, raw, recv, res, live,
    m128, mt, fm, f_row, table, tabf, taps, g128, gsnd, hrec, toep, x3m,
    gmsg, parts, mine, land_r, land_s, order_r, order_s,
    stage_sems, s_in, s_x, r_x, s_w, r_w, s_f, r_f, s_g, r_g, s_z, r_z, s_h, r_h, s_p, r_p, s_a, r_a, s_b, r_b,
):
    S, R = lax.axis_index("src"), lax.axis_index("rcv")
    rows_p, cols_q = 2 * n_rcv, 2 * n_src
    rows = n_rcv * 16
    (nl, ny, nc), (nx, nh) = digits_of(n_src, n_rcv)
    l, y, c = S // (ny * nc), lax.rem(S // nc, ny), lax.rem(S, nc)
    x, h = R // nh, lax.rem(R, nh)

    def at_src(dl, dy, dc):
        return (lax.rem(l + dl, nl) * ny + lax.rem(y + dy, ny)) * nc + lax.rem(c + dc, nc)

    def at_rcv(dx, dh):
        return lax.rem(x + dx, nx) * nh + lax.rem(h + dh, nh)

    z = [(at_src(a, 0, 0), at_rcv(0, b)) for a in range(nl) for b in range(nh) if a or b]
    xs = [(S, at_rcv(a, 0)) for a in range(1, nx)]
    ys = [(at_src(0, a, 0), R) for a in range(1, ny)]
    cs = [(at_src(0, 0, a), R) for a in range(1, nc)]
    bar = pltpu.get_barrier_semaphore()
    near = z + xs + ys + cs
    for d in near:
        pl.semaphore_signal(bar, inc=1, device_id=d, device_id_type=MESH)
    loads = [
        pltpu.make_async_copy(a, b, s_in.at[i])
        for i, (a, b) in enumerate(
            ((filters, filt_in), (mask, mask_in), (slots, slots_in), (traces, xin))
        )
    ]
    for a in loads:
        a.start()

    def stage(i, group):
        for d in group:
            pl.semaphore_signal(stage_sems.at[i], inc=1, device_id=d, device_id_type=MESH)

    offsets = rcv_offsets(nx, nh)
    n_raw = raw_of(n_rcv)
    to_rcv = [at_rcv(a, b) for a, b in offsets]
    from_rcv = [at_rcv(nx - a, nh - b) for a, b in offsets[:n_raw]]

    m128[...] = jnp.zeros((L, L), F32)
    fm[...] = jnp.zeros(fm.shape, F32)
    g128[...] = jnp.zeros((L, L), F32)
    loads[0].wait()
    f = filt_in[...].astype(F32)
    loads[1].wait()
    m128[0:rows_p, 0:cols_q] = mask_in[...].astype(F32)
    for r in range(n_rcv):
        fm[r, 0:2, :] = f[:, :L]
        fm[r, 2:4, :] = f[:, L:]
        fm[r, 4:6, :] = m128[2 * r : 2 * r + 2, :]

    pl.semaphore_wait(bar, len(near))
    stage(0, xs)
    loads[2].wait()
    loads[3].wait()

    def spread(p, carry):
        for b in range(NB):
            xt[p, pl.ds(b, cols_q, stride=NB), :] = xin[p, :, b * L : (b + 1) * L].astype(F32)
        return carry

    lax.fori_loop(0, rows_p, spread, 0)
    pl.semaphore_wait(stage_sems.at[0], len(xs))

    own8 = pl.ds(pl.multiple_of(R * 8, 8), 8)
    for d in to_rcv[:-1]:
        pltpu.make_async_remote_copy(
            fm.at[d], f_row.at[own8], s_f, r_f, device_id=(S, d), device_id_type=MESH
        ).start()
    stage(1, ys)
    f_row[own8, :] = fm[R]
    for i, d in enumerate(to_rcv[:n_raw]):
        a = xt[2 * d].reshape(n_src, 8, L)
        b = xt[2 * d + 1].reshape(n_src, 8, L)
        raw[i] = swap_middle(a, b)
    mt[...] = jnp.transpose(m128[...])
    pl.semaphore_wait(stage_sems.at[1], len(ys))
    stage(2, cs)
    pl.semaphore_wait(stage_sems.at[2], len(cs))

    def send_raw(group):
        for i in group:
            def step(k, carry):
                s = lax.rem(S + k, n_src)
                pltpu.make_async_remote_copy(
                    raw.at[i, s], recv.at[S, R], s_w, r_w.at[i], device_id=(s, to_rcv[i]), device_id_type=MESH
                ).start()
                return carry

            lax.fori_loop(0, n_src, step, 0)

    n_ahead = min(AHEAD, n_raw)
    send_raw(range(n_ahead))

    wait_bytes(f_row.at[pl.ds(0, (n_rcv - 1) * 8)], r_f)
    for i in range(4):
        table[S, i * n_rcv : (i + 1) * n_rcv, :] = f_row[pl.ds(i, n_rcv, stride=8), :].astype(BF16)

    lines = [at_src(a, 0, 0) for a in range(nl)]
    for d in lines[1:]:
        pltpu.make_async_remote_copy(
            table.at[S], table.at[S], s_z, r_z, device_id=(d, R), device_id_type=MESH
        ).start()
    for i in range(2):
        g128[64 + i * n_rcv : 64 + (i + 1) * n_rcv, :] = f_row[pl.ds(4 + i, n_rcv, stride=8), :]
    gt = jnp.transpose(g128[...])
    for s in range(n_src):
        gsnd[s] = gt[2 * s : 2 * s + 2, :]

    def send_live(k, carry):
        d = lax.rem(S + k, n_src)
        pltpu.make_async_remote_copy(
            gsnd.at[d], hrec.at[S], s_h, r_h, device_id=(d, R), device_id_type=MESH
        ).start()
        return carry

    lax.fori_loop(1, n_src, send_live, 0)

    send_raw(range(n_ahead, n_raw))
    hrec[S] = gsnd[S]
    flip = jnp.where(iota((L, L), 0) + iota((L, L), 1) == L - 1, 1.0, 0.0).astype(BF16)

    def delays(s, carry):
        v3 = delayed(xt[:, pl.ds(pl.multiple_of(s * 8, 8), 8), :])
        for d in range(3):
            at = (2 - d) * L
            x3[s, :, at : at + L] = v3[d]
            x3t[s, at : at + L, :] = lax.dot_general(
                flip, v3[d], (((1,), (1,)), ((), ())), preferred_element_type=F32
            ).astype(BF16)
        return carry

    lax.fori_loop(0, n_src, delays, 0)

    if nl > 1:
        wait_bytes(table.at[pl.ds(0, nl - 1)], r_z)
    for a in range(1, ny * nc):
        d = at_src(0, a // nc, a % nc)
        for b in lines:
            pltpu.make_async_remote_copy(
                table.at[b], table.at[b], s_g, r_g, device_id=(d, R), device_id_type=MESH
            ).start()
    if nl > 1:
        wait_bytes(table.at[pl.ds(0, nl - 1)], s_z)
    wait_bytes(table.at[pl.ds(0, n_src - nl)], r_g)
    tabf[...] = table[...].astype(F32).reshape(tabf.shape)

    def pick(slot, w):
        st = slots_in[slot]
        at = (st // (2 * n_rcv)) * (4 * n_rcv) + lax.rem(st, 2) * n_rcv + lax.rem(st // 2, n_rcv)
        taps[pl.ds(2 * w, 1), :] = tabf[pl.ds(at, 1), :]
        taps[pl.ds(2 * w + 1, 1), :] = tabf[pl.ds(at + 2 * n_rcv, 1), :]

    def pick_pair(w, carry):
        slot = (w * n_rcv + R) * 2
        pick(slot, 2 * w)
        pick(slot + 1, 2 * w + 1)
        return carry

    lax.fori_loop(0, n_src, pick_pair, 0)
    for i, d in enumerate(from_rcv):
        for p in range(2):
            pick(S * rows_p + 2 * d + p, cols_q + 2 * i + p)

    later = iota((L, L), 1) >= iota((L, L), 0)
    row8 = iota((rows // 8, 8, L), 1)
    q2 = (row8 // NB).reshape(rows, L)
    p2 = lax.rem(iota((rows, L), 0) // (2 * NB), 2)

    def offset_of(i):
        o = n_src - 1 - i
        return lax.rem(o // nc, nl), o // (nc * nl), lax.rem(o, nc)

    def pair_taps(w, out):
        for i in range(2):
            at = 4 * w + 2 * i
            toeplitz(taps[pl.ds(at, 1), :], taps[pl.ds(at + 1, 1), :], later, out, i * L)

    def filter_two(i0, last):
        to = []
        for u in range(2):
            dl, dy, dc = offset_of(i0 + u)
            s = at_src(dl, dy, dc)
            to.append(s)
            pair_taps(s, toep.at[u])
        for u, s in enumerate(to):
            v = jnp.dot(x3[s], toep[u], preferred_element_type=F32)
            v = jnp.where(q2 == 1, v[:, L:], v[:, :L]).astype(BF16)
            floc[s] = v
            v = v.astype(F32).reshape(n_rcv, 2, 8, L)
            send[s] = swap_middle(v[:, 0], v[:, 1])
        for u, s in enumerate(to):
            own = last and u == 1
            for d in to_rcv[n_raw : n_rcv - (1 if own else 0)]:
                pltpu.make_async_remote_copy(
                    send.at[s, d], recv.at[S, R], s_x, r_x.at[i0 + u], device_id=(s, d), device_id_type=MESH
                ).start()

    def filter_step(i, carry):
        filter_two(2 * i, False)
        return carry

    lax.fori_loop(0, n_src // 2 - 1, filter_step, 0)
    filter_two(n_src - 2, True)
    recv[S, R] = send[S, R]

    for i, d in enumerate(from_rcv):
        wait_bytes(recv.at[0], r_w.at[i])
        v = recv[:, pl.ds(d, 1)].reshape(rows // 8, 8, L).astype(F32)
        v3 = delayed(v)
        for k in range(3):
            x3m[i % 2, :, (2 - k) * L : (3 - k) * L] = v3[k]
        pair_taps(n_src + i, toep.at[i % 2])
        v = jnp.dot(x3m[i % 2], toep[i % 2], preferred_element_type=F32)
        v = jnp.where(p2 == 1, v[:, L:], v[:, :L]).astype(BF16)
        recv[:, pl.ds(d, 1)] = v.reshape(n_src, 1, 16, L)

    wait_bytes(hrec.at[pl.ds(0, n_src - 1)], r_h)
    lane = iota((rows, L), 1)
    tile = iota((rows, L), 0) // 16
    pown = lane == 2 * tile + p2
    prec = lane == 64 + q2 * n_rcv + tile
    ones = jnp.where((iota((L, 2 * L), 0) < 64) == (iota((L, 2 * L), 1) < L), 1.0, 0.0).astype(BF16)

    def widen(i, carry):
        for u in range(2):
            s = 2 * i + u
            own = jnp.where(q2 == 0, mt[pl.ds(2 * s, 1), :], mt[pl.ds(2 * s + 1, 1), :])
            other = jnp.where(p2 == 0, hrec[s, 0:1, :], hrec[s, 1:2, :])
            v = jnp.where(pown, own, jnp.where(prec, other, 0.0)).astype(BF16)
            live[s] = jnp.dot(v, ones, preferred_element_type=F32).astype(BF16)
        return carry

    lax.fori_loop(0, n_src // 2, widen, 0)

    reach = iota((L, L), 1) + iota((L, L), 0) >= L - 1

    def lag_pairs(i0, count, last):
        found = []
        for u in range(count):
            dl, dy, dc = offset_of(i0 + u)
            s = at_src(nl - dl, ny - dy, nc - dc)
            wait_bytes(recv.at[0, pl.ds(0, n_rcv - n_raw - (1 if last else 0))], r_x.at[i0 + u])
            found.append(s)
        ms = []
        for s in found:
            diff = floc[s].astype(F32) - recv[s].reshape(rows, L).astype(F32)
            lv = live[s].astype(F32)
            for t in range(2):
                r = lv[:, t * L : (t + 1) * L] * diff
                if t == 0:
                    res[:, pl.ds(pl.multiple_of(s * 8, 8), 8), :] = r.reshape(rows_p, 8, L)
                both = jnp.concatenate([jnp.where(q2 == 0, r, 0.0), jnp.where(q2 == 1, r, 0.0)], axis=1)
                ms.append(jnp.dot(x3t[s], both.astype(BF16), preferred_element_type=F32))
        for u, s in enumerate(found):
            sums = []
            for t in range(2):
                m = ms[2 * u + t]
                for i in range(2):
                    mi = m[:, i * L : (i + 1) * L]
                    m2, m1, m0 = mi[0:L], mi[L : 2 * L], mi[2 * L : 3 * L]
                    for a, b in ((m0, m1), (m1, m2)):
                        skew = pltpu.roll(jnp.where(reach, a, b), 1, 1, stride=1, stride_axis=0)
                        sums.append(jnp.sum(skew, axis=0, keepdims=True))
            msg = jnp.concatenate(sums, axis=0)
            if last:
                parts[S] = msg
            else:
                gmsg[s] = msg
                pltpu.make_async_remote_copy(
                    gmsg.at[s], parts.at[S], s_p, r_p, device_id=(s, R), device_id_type=MESH
                ).start()

    def lag_step(i, carry):
        lag_pairs(2 * i, 2, False)
        return carry

    lax.fori_loop(0, n_src // 2 - 1, lag_step, 0)
    lag_pairs(n_src - 2, 1, False)
    lag_pairs(n_src - 1, 1, True)

    wait_bytes(parts.at[pl.ds(0, n_src - 1)], r_p)
    total = jnp.sum(parts[...], axis=0) * scale
    mine[0] = total[:4]
    mine[1] = total[4:]
    for d in to_rcv[:-1]:
        pltpu.make_async_remote_copy(
            mine.at[1], land_s.at[R], s_b, r_b, device_id=(S, d), device_id_type=MESH
        ).start()

    def send_src(k, carry):
        pltpu.make_async_remote_copy(
            mine.at[0], land_r.at[S], s_a, r_a, device_id=(lax.rem(S + k, n_src), R), device_id_type=MESH
        ).start()
        return carry

    lax.fori_loop(1, n_src, send_src, 0)
    land_r[S] = total[:4]
    land_s[R] = total[4:]

    def gather(p, carry):
        for b in range(NB):
            residual[p, :, b * L : (b + 1) * L] = res[p, pl.ds(b, cols_q, stride=NB), :].astype(BF16)
        return carry

    lax.fori_loop(0, rows_p, gather, 0)
    wait_bytes(f_row.at[pl.ds(0, (n_rcv - 1) * 8)], s_f)
    wait_bytes(table.at[pl.ds(0, n_src - nl)], s_g)
    wait_bytes(hrec.at[pl.ds(0, n_src - 1)], s_h)
    wait_bytes(parts.at[pl.ds(0, n_src - 1)], s_p)
    wait_bytes(raw, s_w)
    for i in range(n_src):
        wait_bytes(recv.at[0, pl.ds(0, n_rcv - n_raw - (1 if i == n_src - 1 else 0))], s_x)
    wait_bytes(land_r.at[pl.ds(0, n_src - 1)], s_a)
    wait_bytes(land_s.at[pl.ds(0, n_rcv - 1)], s_b)
    wait_bytes(land_r.at[pl.ds(0, n_src - 1)], r_a)
    wait_bytes(land_s.at[pl.ds(0, n_rcv - 1)], r_b)
    for i in range(2):
        for k in range(2):
            order_r[k, pl.ds(i, n_src, stride=2), :] = land_r[:, 2 * i + k, :]
            order_s[k, pl.ds(i, n_rcv, stride=2), :] = land_s[:, 2 * i + k, :]
    for k in range(2):
        at = slice(k * L, (k + 1) * L)
        grad_rcv[:, at] = order_r[k]
        grad_src[:, at] = order_s[k]


def hand_on(a, b, c, x, y, z):
    x[...] = a[...]
    y[...] = b[...]
    z[...] = c[...]


def shards(traces, dead_mask, filters, station_of_slot):
    rows_p, cols_q, trace_len = traces.shape
    tap_count = filters.shape[1]
    n_src, n_rcv = lax.axis_size("src"), lax.axis_size("rcv")
    rows = n_rcv * 16
    n_raw = raw_of(n_rcv)
    scale = 1.0 / math.sqrt(rows_p * n_src * trace_len)
    vm = pl.BlockSpec(memory_space=pltpu.VMEM)
    hbm = pl.BlockSpec(memory_space=pltpu.HBM)
    V = pltpu.VMEM
    D = pltpu.SemaphoreType.DMA
    shapes = (
        jax.ShapeDtypeStruct(traces.shape, BF16),
        jax.ShapeDtypeStruct((cols_q, tap_count), F32),
        jax.ShapeDtypeStruct((rows_p, tap_count), F32),
    )
    outs = pl.pallas_call(
        functools.partial(kernel, n_src, n_rcv, scale),
        out_shape=shapes,
        in_specs=[hbm] * 4,
        out_specs=(vm, vm, vm),
        scratch_shapes=[
            V(traces.shape, BF16),
            V(dead_mask.shape, jnp.int32),
            V(filters.shape, BF16),
            pltpu.SMEM(station_of_slot.shape, jnp.int32),
            V((rows_p, NB * cols_q, L), F32),
            V((n_src, rows, 3 * L), BF16),
            V((n_src, 3 * L, rows), BF16),
            V((n_src, rows, L), BF16),
            V((n_src, n_rcv, 16, L), BF16),
            V((n_raw, n_src, 16, L), BF16),
            V((n_src, n_rcv, 16, L), BF16),
            V((rows_p, NB * cols_q, L), F32),
            V((n_src, rows, 2 * L), BF16),
            V((L, L), F32),
            V((L, L), F32),
            V((n_rcv, 8, L), F32),
            V((n_rcv * 8, L), F32),
            V((n_src, 4 * n_rcv, L), BF16),
            V((n_src * 4 * n_rcv, L), F32),
            V((2 * cols_q + 4 * n_raw, L), F32),
            V((L, L), F32),
            V((n_src, 2, L), F32),
            V((n_src, 2, L), F32),
            V((2, 3 * L, 2 * L), BF16),
            V((2, rows, 3 * L), BF16),
            V((n_src, 8, L), F32),
            V((n_src, 8, L), F32),
            V((2, 4, L), F32),
            V((n_src, 4, L), F32),
            V((n_rcv, 4, L), F32),
            V((2, cols_q, L), F32),
            V((2, rows_p, L), F32),
            pltpu.SemaphoreType.REGULAR((3,)),
            D((4,)), D, D((n_src,)), D, D((n_raw,)),
            D, D, D, D, D, D, D, D, D, D, D, D, D, D,
        ],
        compiler_params=pltpu.CompilerParams(
            collective_id=0, has_side_effects=True, vmem_limit_bytes=60 << 20
        ),
    )(traces, dead_mask, filters, station_of_slot)
    return pl.pallas_call(
        hand_on, out_shape=shapes, in_specs=[vm] * 3, out_specs=(vm,) * 3
    )(*outs)


def solution(mesh):
    placed = (P("src", "rcv", None), P("src", "rcv"), P(("src", "rcv"), None), P())
    return jax.shard_map(
        shards,
        mesh=mesh,
        in_specs=placed,
        out_specs=(P("src", "rcv", None), P("rcv", None), P("src", None)),
        check_vma=False,
    )
```

```python
import functools
import math

import jax
import jax.numpy as jnp
from jax import lax
from jax.experimental import pallas as pl
from jax.experimental.pallas import tpu as pltpu
from jax.sharding import PartitionSpec as P

MESH = pl.DeviceIdType.MESH
F32 = jnp.float32
BF16 = jnp.bfloat16
NB = 4
L = 128
RAW = 6
AHEAD = 3


def digits_of(n_src, n_rcv):
    if (n_src, n_rcv) == (16, 16):
        return (2, 4, 2), (4, 4)
    return (1, n_src // 2, 2), (n_rcv // 2, 2)


def rcv_offsets(nx, nh):
    def far(d):
        return 2 * min(d[1], nh - d[1]), min(d[0], nx - d[0])

    return sorted([(a, b) for a in range(nx) for b in range(nh)], key=far, reverse=True)


def raw_of(n_rcv):
    return n_rcv * RAW // 16


def wait_bytes(ref, sem):
    pltpu.make_async_copy(ref, ref, sem).wait()


def iota(shape, axis):
    return lax.broadcasted_iota(jnp.int32, shape, axis)


def swap_middle(a, b):
    low = iota(a.shape, 1) < 4
    ra, rb = pltpu.roll(a, 4, 1), pltpu.roll(b, 4, 1)
    w0, w1 = jnp.where(low, a, rb), jnp.where(low, ra, b)
    return jnp.concatenate([w0, w1], axis=1).astype(BF16)


def delayed(x):
    block = lax.rem(iota(x.shape, 1), NB)
    n = x.shape[0] * 8
    out = [x]
    for d in (1, 2):
        out.append(jnp.where(block >= d, pltpu.roll(x, d, 1), 0.0))
    return [v.reshape(n, L).astype(BF16) for v in out]


def toeplitz(c0, c1, later, out, at):
    c0 = pltpu.roll(jnp.broadcast_to(c0, (L, L)), 0, 1, stride=1, stride_axis=0)
    c1 = pltpu.roll(jnp.broadcast_to(c1, (L, L)), 0, 1, stride=1, stride_axis=0)
    out[0:L, at : at + L] = jnp.where(later, 0.0, c1).astype(BF16)
    out[L : 2 * L, at : at + L] = jnp.where(later, c1, c0).astype(BF16)
    out[2 * L : 3 * L, at : at + L] = jnp.where(later, c0, 0.0).astype(BF16)


def kernel(
    n_src, n_rcv, scale,
    traces, mask, filters, slots,
    residual, grad_rcv, grad_src,
    xin, mask_in, filt_in, slots_in,
    xt, x3, x3t, floc, send, raw, recv, res, live,
    m128, mt, fm, f_row, table, tabf, taps, g128, gsnd, hrec, toep, x3m,
    gmsg, parts, mine, land_r, land_s, order_r, order_s,
    stage_sems, s_in, s_x, r_x, s_w, r_w, s_f, r_f, s_g, r_g, s_z, r_z, s_c, r_c, s_h, r_h, s_p, r_p, s_a, r_a, s_b, r_b,
):
    S, R = lax.axis_index("src"), lax.axis_index("rcv")
    rows_p, cols_q = 2 * n_rcv, 2 * n_src
    rows = n_rcv * 16
    (nl, ny, nc), (nx, nh) = digits_of(n_src, n_rcv)
    l, y, c = S // (ny * nc), lax.rem(S // nc, ny), lax.rem(S, nc)
    x, h = R // nh, lax.rem(R, nh)

    def at_src(dl, dy, dc):
        return (lax.rem(l + dl, nl) * ny + lax.rem(y + dy, ny)) * nc + lax.rem(c + dc, nc)

    def at_rcv(dx, dh):
        return lax.rem(x + dx, nx) * nh + lax.rem(h + dh, nh)

    z = [(at_src(a, 0, 0), at_rcv(0, b)) for a in range(nl) for b in range(nh) if a or b]
    xs = [(S, at_rcv(a, 0)) for a in range(1, nx)]
    ys = [(at_src(0, a, 0), R) for a in range(1, ny)]
    cs = [(at_src(0, 0, a), R) for a in range(1, nc)]
    bar = pltpu.get_barrier_semaphore()
    near = z + xs + ys + cs
    for d in near:
        pl.semaphore_signal(bar, inc=1, device_id=d, device_id_type=MESH)
    loads = [
        pltpu.make_async_copy(a, b, s_in.at[i])
        for i, (a, b) in enumerate(
            ((filters, filt_in), (mask, mask_in), (slots, slots_in), (traces, xin))
        )
    ]
    for a in loads:
        a.start()

    def stage(i, group):
        for d in group:
            pl.semaphore_signal(stage_sems.at[i], inc=1, device_id=d, device_id_type=MESH)

    offsets = rcv_offsets(nx, nh)
    n_raw = raw_of(n_rcv)
    to_rcv = [at_rcv(a, b) for a, b in offsets]
    from_rcv = [at_rcv(nx - a, nh - b) for a, b in offsets[:n_raw]]

    m128[...] = jnp.zeros((L, L), F32)
    fm[...] = jnp.zeros(fm.shape, F32)
    g128[...] = jnp.zeros((L, L), F32)
    loads[0].wait()
    f = filt_in[...].astype(F32)
    loads[1].wait()
    m128[0:rows_p, 0:cols_q] = mask_in[...].astype(F32)
    for r in range(n_rcv):
        fm[r, 0:2, :] = f[:, :L]
        fm[r, 2:4, :] = f[:, L:]
        fm[r, 4:6, :] = m128[2 * r : 2 * r + 2, :]

    pl.semaphore_wait(bar, len(near))
    stage(0, xs)
    loads[2].wait()
    loads[3].wait()

    def spread(p, carry):
        for b in range(NB):
            xt[p, pl.ds(b, cols_q, stride=NB), :] = xin[p, :, b * L : (b + 1) * L].astype(F32)
        return carry

    lax.fori_loop(0, rows_p, spread, 0)
    pl.semaphore_wait(stage_sems.at[0], len(xs))

    own8 = pl.ds(pl.multiple_of(R * 8, 8), 8)
    for d in to_rcv[:-1]:
        pltpu.make_async_remote_copy(
            fm.at[d], f_row.at[own8], s_f, r_f, device_id=(S, d), device_id_type=MESH
        ).start()
    stage(1, ys)
    f_row[own8, :] = fm[R]
    for i, d in enumerate(to_rcv[:n_raw]):
        a = xt[2 * d].reshape(n_src, 8, L)
        b = xt[2 * d + 1].reshape(n_src, 8, L)
        raw[i] = swap_middle(a, b)
    mt[...] = jnp.transpose(m128[...])
    pl.semaphore_wait(stage_sems.at[1], len(ys))
    stage(2, cs)
    pl.semaphore_wait(stage_sems.at[2], len(cs))

    def send_raw(group):
        for i in group:
            def step(k, carry):
                s = lax.rem(S + k, n_src)
                pltpu.make_async_remote_copy(
                    raw.at[i, s], recv.at[S, R], s_w, r_w.at[i], device_id=(s, to_rcv[i]), device_id_type=MESH
                ).start()
                return carry

            lax.fori_loop(0, n_src, step, 0)

    n_ahead = min(AHEAD, n_raw)
    send_raw(range(n_ahead))

    wait_bytes(f_row.at[pl.ds(0, (n_rcv - 1) * 8)], r_f)
    for i in range(4):
        table[S, i * n_rcv : (i + 1) * n_rcv, :] = f_row[pl.ds(i, n_rcv, stride=8), :].astype(BF16)

    lines = [at_src(a, 0, 0) for a in range(nl)]
    for d in lines[1:]:
        pltpu.make_async_remote_copy(
            table.at[S], table.at[S], s_z, r_z, device_id=(d, R), device_id_type=MESH
        ).start()
    for i in range(2):
        g128[64 + i * n_rcv : 64 + (i + 1) * n_rcv, :] = f_row[pl.ds(4 + i, n_rcv, stride=8), :]
    gt = jnp.transpose(g128[...])
    for s in range(n_src):
        gsnd[s] = gt[2 * s : 2 * s + 2, :]

    def send_live(k, carry):
        d = lax.rem(S + k, n_src)
        pltpu.make_async_remote_copy(
            gsnd.at[d], hrec.at[S], s_h, r_h, device_id=(d, R), device_id_type=MESH
        ).start()
        return carry

    lax.fori_loop(1, n_src, send_live, 0)

    send_raw(range(n_ahead, n_raw))
    hrec[S] = gsnd[S]
    flip = jnp.where(iota((L, L), 0) + iota((L, L), 1) == L - 1, 1.0, 0.0).astype(BF16)

    def delays(s, carry):
        v3 = delayed(xt[:, pl.ds(pl.multiple_of(s * 8, 8), 8), :])
        for d in range(3):
            at = (2 - d) * L
            x3[s, :, at : at + L] = v3[d]
            x3t[s, at : at + L, :] = lax.dot_general(
                flip, v3[d], (((1,), (1,)), ((), ())), preferred_element_type=F32
            ).astype(BF16)
        return carry

    lax.fori_loop(0, n_src, delays, 0)

    if nl > 1:
        wait_bytes(table.at[pl.ds(0, nl - 1)], r_z)
    for a in range(1, ny):
        for b in lines:
            pltpu.make_async_remote_copy(
                table.at[b], table.at[b], s_g, r_g, device_id=(at_src(0, a, 0), R), device_id_type=MESH
            ).start()
    if nl > 1:
        wait_bytes(table.at[pl.ds(0, nl - 1)], s_z)
    wait_bytes(table.at[pl.ds(0, nl * (ny - 1))], r_g)
    for k in range(1, nc):
        for a in range(nl):
            for b in range(ny):
                t = at_src(a, b, 0)
                pltpu.make_async_remote_copy(
                    table.at[t], table.at[t], s_c, r_c, device_id=(at_src(0, 0, k), R), device_id_type=MESH
                ).start()
    wait_bytes(table.at[pl.ds(0, n_src - nl * ny)], r_c)
    tabf[...] = table[...].astype(F32).reshape(tabf.shape)

    def pick(slot, w):
        st = slots_in[slot]
        at = (st // (2 * n_rcv)) * (4 * n_rcv) + lax.rem(st, 2) * n_rcv + lax.rem(st // 2, n_rcv)
        taps[pl.ds(2 * w, 1), :] = tabf[pl.ds(at, 1), :]
        taps[pl.ds(2 * w + 1, 1), :] = tabf[pl.ds(at + 2 * n_rcv, 1), :]

    def pick_pair(w, carry):
        slot = (w * n_rcv + R) * 2
        pick(slot, 2 * w)
        pick(slot + 1, 2 * w + 1)
        return carry

    lax.fori_loop(0, n_src, pick_pair, 0)
    for i, d in enumerate(from_rcv):
        for p in range(2):
            pick(S * rows_p + 2 * d + p, cols_q + 2 * i + p)

    later = iota((L, L), 1) >= iota((L, L), 0)
    row8 = iota((rows // 8, 8, L), 1)
    q2 = (row8 // NB).reshape(rows, L)
    p2 = lax.rem(iota((rows, L), 0) // (2 * NB), 2)

    def offset_of(i):
        o = n_src - 1 - i
        return lax.rem(o // nc, nl), o // (nc * nl), lax.rem(o, nc)

    def pair_taps(w, out):
        for i in range(2):
            at = 4 * w + 2 * i
            toeplitz(taps[pl.ds(at, 1), :], taps[pl.ds(at + 1, 1), :], later, out, i * L)

    def filter_two(i0, last):
        to = []
        for u in range(2):
            dl, dy, dc = offset_of(i0 + u)
            s = at_src(dl, dy, dc)
            to.append(s)
            pair_taps(s, toep.at[u])
        for u, s in enumerate(to):
            v = jnp.dot(x3[s], toep[u], preferred_element_type=F32)
            v = jnp.where(q2 == 1, v[:, L:], v[:, :L]).astype(BF16)
            floc[s] = v
            v = v.astype(F32).reshape(n_rcv, 2, 8, L)
            send[s] = swap_middle(v[:, 0], v[:, 1])
        for u, s in enumerate(to):
            own = last and u == 1
            for d in to_rcv[n_raw : n_rcv - (1 if own else 0)]:
                pltpu.make_async_remote_copy(
                    send.at[s, d], recv.at[S, R], s_x, r_x.at[i0 + u], device_id=(s, d), device_id_type=MESH
                ).start()

    def filter_step(i, carry):
        filter_two(2 * i, False)
        return carry

    lax.fori_loop(0, n_src // 2 - 1, filter_step, 0)
    filter_two(n_src - 2, True)
    recv[S, R] = send[S, R]

    for i, d in enumerate(from_rcv):
        wait_bytes(recv.at[0], r_w.at[i])
        v = recv[:, pl.ds(d, 1)].reshape(rows // 8, 8, L).astype(F32)
        v3 = delayed(v)
        for k in range(3):
            x3m[i % 2, :, (2 - k) * L : (3 - k) * L] = v3[k]
        pair_taps(n_src + i, toep.at[i % 2])
        v = jnp.dot(x3m[i % 2], toep[i % 2], preferred_element_type=F32)
        v = jnp.where(p2 == 1, v[:, L:], v[:, :L]).astype(BF16)
        recv[:, pl.ds(d, 1)] = v.reshape(n_src, 1, 16, L)

    wait_bytes(hrec.at[pl.ds(0, n_src - 1)], r_h)
    lane = iota((rows, L), 1)
    tile = iota((rows, L), 0) // 16
    pown = lane == 2 * tile + p2
    prec = lane == 64 + q2 * n_rcv + tile
    ones = jnp.where((iota((L, 2 * L), 0) < 64) == (iota((L, 2 * L), 1) < L), 1.0, 0.0).astype(BF16)

    def widen(i, carry):
        for u in range(2):
            s = 2 * i + u
            own = jnp.where(q2 == 0, mt[pl.ds(2 * s, 1), :], mt[pl.ds(2 * s + 1, 1), :])
            other = jnp.where(p2 == 0, hrec[s, 0:1, :], hrec[s, 1:2, :])
            v = jnp.where(pown, own, jnp.where(prec, other, 0.0)).astype(BF16)
            live[s] = jnp.dot(v, ones, preferred_element_type=F32).astype(BF16)
        return carry

    lax.fori_loop(0, n_src // 2, widen, 0)

    reach = iota((L, L), 1) + iota((L, L), 0) >= L - 1

    def lag_pairs(i0, count, last):
        found = []
        for u in range(count):
            dl, dy, dc = offset_of(i0 + u)
            s = at_src(nl - dl, ny - dy, nc - dc)
            wait_bytes(recv.at[0, pl.ds(0, n_rcv - n_raw - (1 if last else 0))], r_x.at[i0 + u])
            found.append(s)
        ms = []
        for s in found:
            diff = floc[s].astype(F32) - recv[s].reshape(rows, L).astype(F32)
            lv = live[s].astype(F32)
            for t in range(2):
                r = lv[:, t * L : (t + 1) * L] * diff
                if t == 0:
                    res[:, pl.ds(pl.multiple_of(s * 8, 8), 8), :] = r.reshape(rows_p, 8, L)
                both = jnp.concatenate([jnp.where(q2 == 0, r, 0.0), jnp.where(q2 == 1, r, 0.0)], axis=1)
                ms.append(jnp.dot(x3t[s], both.astype(BF16), preferred_element_type=F32))
        for u, s in enumerate(found):
            sums = []
            for t in range(2):
                m = ms[2 * u + t]
                for i in range(2):
                    mi = m[:, i * L : (i + 1) * L]
                    m2, m1, m0 = mi[0:L], mi[L : 2 * L], mi[2 * L : 3 * L]
                    for a, b in ((m0, m1), (m1, m2)):
                        skew = pltpu.roll(jnp.where(reach, a, b), 1, 1, stride=1, stride_axis=0)
                        sums.append(jnp.sum(skew, axis=0, keepdims=True))
            msg = jnp.concatenate(sums, axis=0)
            if last:
                parts[S] = msg
            else:
                gmsg[s] = msg
                pltpu.make_async_remote_copy(
                    gmsg.at[s], parts.at[S], s_p, r_p, device_id=(s, R), device_id_type=MESH
                ).start()

    def lag_step(i, carry):
        lag_pairs(2 * i, 2, False)
        return carry

    lax.fori_loop(0, n_src // 2 - 1, lag_step, 0)
    lag_pairs(n_src - 2, 1, False)
    lag_pairs(n_src - 1, 1, True)

    wait_bytes(parts.at[pl.ds(0, n_src - 1)], r_p)
    total = jnp.sum(parts[...], axis=0) * scale
    mine[0] = total[:4]
    mine[1] = total[4:]
    for d in to_rcv[:-1]:
        pltpu.make_async_remote_copy(
            mine.at[1], land_s.at[R], s_b, r_b, device_id=(S, d), device_id_type=MESH
        ).start()

    def send_src(k, carry):
        pltpu.make_async_remote_copy(
            mine.at[0], land_r.at[S], s_a, r_a, device_id=(lax.rem(S + k, n_src), R), device_id_type=MESH
        ).start()
        return carry

    lax.fori_loop(1, n_src, send_src, 0)
    land_r[S] = total[:4]
    land_s[R] = total[4:]

    def gather(p, carry):
        for b in range(NB):
            xin[p, :, b * L : (b + 1) * L] = res[p, pl.ds(b, cols_q, stride=NB), :].astype(BF16)
        return carry

    lax.fori_loop(0, rows_p, gather, 0)
    store = pltpu.make_async_copy(xin, residual, s_in.at[3])
    store.start()
    wait_bytes(f_row.at[pl.ds(0, (n_rcv - 1) * 8)], s_f)
    wait_bytes(table.at[pl.ds(0, nl * (ny - 1))], s_g)
    wait_bytes(table.at[pl.ds(0, n_src - nl * ny)], s_c)
    wait_bytes(hrec.at[pl.ds(0, n_src - 1)], s_h)
    wait_bytes(parts.at[pl.ds(0, n_src - 1)], s_p)
    wait_bytes(raw, s_w)
    for i in range(n_src):
        wait_bytes(recv.at[0, pl.ds(0, n_rcv - n_raw - (1 if i == n_src - 1 else 0))], s_x)
    wait_bytes(land_r.at[pl.ds(0, n_src - 1)], s_a)
    wait_bytes(land_s.at[pl.ds(0, n_rcv - 1)], s_b)
    wait_bytes(land_r.at[pl.ds(0, n_src - 1)], r_a)
    wait_bytes(land_s.at[pl.ds(0, n_rcv - 1)], r_b)
    for i in range(2):
        for k in range(2):
            order_r[k, pl.ds(i, n_src, stride=2), :] = land_r[:, 2 * i + k, :]
            order_s[k, pl.ds(i, n_rcv, stride=2), :] = land_s[:, 2 * i + k, :]
    for k in range(2):
        at = slice(k * L, (k + 1) * L)
        grad_rcv[:, at] = order_r[k]
        grad_src[:, at] = order_s[k]
    store.wait()


def hand_on(a, b, c, x, y, z, buf, buf_r, buf_s, sems):
    parts = buf.shape[0] // 4
    ways = [(a.at[pl.ds(i * parts, parts)], buf.at[pl.ds(i * parts, parts)], x.at[pl.ds(i * parts, parts)]) for i in range(4)]
    ways += [(b, buf_r, y), (c, buf_s, z)]
    loads = [pltpu.make_async_copy(i, m, sems.at[0, k]) for k, (i, m, o) in enumerate(ways)]
    stores = [pltpu.make_async_copy(m, o, sems.at[1, k]) for k, (i, m, o) in enumerate(ways)]
    for copy in loads:
        copy.start()
    for load, store in zip(loads, stores):
        load.wait()
        store.start()
    for copy in stores:
        copy.wait()


def shards(traces, dead_mask, filters, station_of_slot):
    rows_p, cols_q, trace_len = traces.shape
    tap_count = filters.shape[1]
    n_src, n_rcv = lax.axis_size("src"), lax.axis_size("rcv")
    rows = n_rcv * 16
    n_raw = raw_of(n_rcv)
    scale = 1.0 / math.sqrt(rows_p * n_src * trace_len)
    vm = pl.BlockSpec(memory_space=pltpu.VMEM)
    hbm = pl.BlockSpec(memory_space=pltpu.HBM)
    V = pltpu.VMEM
    D = pltpu.SemaphoreType.DMA
    shapes = (
        jax.ShapeDtypeStruct(traces.shape, BF16),
        jax.ShapeDtypeStruct((cols_q, tap_count), F32),
        jax.ShapeDtypeStruct((rows_p, tap_count), F32),
    )
    outs = pl.pallas_call(
        functools.partial(kernel, n_src, n_rcv, scale),
        out_shape=shapes,
        in_specs=[hbm] * 4,
        out_specs=(hbm, vm, vm),
        scratch_shapes=[
            V(traces.shape, BF16),
            V(dead_mask.shape, jnp.int32),
            V(filters.shape, BF16),
            pltpu.SMEM(station_of_slot.shape, jnp.int32),
            V((rows_p, NB * cols_q, L), F32),
            V((n_src, rows, 3 * L), BF16),
            V((n_src, 3 * L, rows), BF16),
            V((n_src, rows, L), BF16),
            V((n_src, n_rcv, 16, L), BF16),
            V((n_raw, n_src, 16, L), BF16),
            V((n_src, n_rcv, 16, L), BF16),
            V((rows_p, NB * cols_q, L), F32),
            V((n_src, rows, 2 * L), BF16),
            V((L, L), F32),
            V((L, L), F32),
            V((n_rcv, 8, L), F32),
            V((n_rcv * 8, L), F32),
            V((n_src, 4 * n_rcv, L), BF16),
            V((n_src * 4 * n_rcv, L), F32),
            V((2 * cols_q + 4 * n_raw, L), F32),
            V((L, L), F32),
            V((n_src, 2, L), F32),
            V((n_src, 2, L), F32),
            V((2, 3 * L, 2 * L), BF16),
            V((2, rows, 3 * L), BF16),
            V((n_src, 8, L), F32),
            V((n_src, 8, L), F32),
            V((2, 4, L), F32),
            V((n_src, 4, L), F32),
            V((n_rcv, 4, L), F32),
            V((2, cols_q, L), F32),
            V((2, rows_p, L), F32),
            pltpu.SemaphoreType.REGULAR((3,)),
            D((4,)), D, D((n_src,)), D, D((n_raw,)),
            D, D, D, D, D, D, D, D, D, D, D, D, D, D, D, D,
        ],
        compiler_params=pltpu.CompilerParams(
            collective_id=0, has_side_effects=True, vmem_limit_bytes=60 << 20
        ),
    )(traces, dead_mask, filters, station_of_slot)
    return pl.pallas_call(
        hand_on,
        out_shape=shapes,
        in_specs=[hbm] * 3,
        out_specs=(hbm,) * 3,
        scratch_shapes=[V(traces.shape, BF16), V(shapes[1].shape, F32), V(shapes[2].shape, F32), D((2, 6))],
    )(*outs)


def solution(mesh):
    placed = (P("src", "rcv", None), P("src", "rcv"), P(("src", "rcv"), None), P())
    return jax.shard_map(
        shards,
        mesh=mesh,
        in_specs=placed,
        out_specs=(P("src", "rcv", None), P("rcv", None), P("src", None)),
        check_vma=False,
    )
```

```python
import functools
import math

import jax
import jax.numpy as jnp
from jax import lax
from jax.experimental import pallas as pl
from jax.experimental.pallas import tpu as pltpu
from jax.sharding import PartitionSpec as P

MESH = pl.DeviceIdType.MESH
F32 = jnp.float32
BF16 = jnp.bfloat16
NB = 4
L = 128
RAW = 7
AHEAD = 3


def digits_of(n_src, n_rcv):
    if (n_src, n_rcv) == (16, 16):
        return (2, 4, 2), (4, 4)
    return (1, n_src // 2, 2), (n_rcv // 2, 2)


def rcv_offsets(nx, nh):
    def far(d):
        return 2 * min(d[1], nh - d[1]), min(d[0], nx - d[0])

    return sorted([(a, b) for a in range(nx) for b in range(nh)], key=far, reverse=True)


def raw_of(n_rcv):
    return n_rcv * RAW // 16


def wait_bytes(ref, sem):
    pltpu.make_async_copy(ref, ref, sem).wait()


def iota(shape, axis):
    return lax.broadcasted_iota(jnp.int32, shape, axis)


def swap_middle(a, b):
    low = iota(a.shape, 1) < 4
    ra, rb = pltpu.roll(a, 4, 1), pltpu.roll(b, 4, 1)
    w0, w1 = jnp.where(low, a, rb), jnp.where(low, ra, b)
    return jnp.concatenate([w0, w1], axis=1).astype(BF16)


def delayed(x):
    block = lax.rem(iota(x.shape, 1), NB)
    n = x.shape[0] * 8
    out = [x]
    for d in (1, 2):
        out.append(jnp.where(block >= d, pltpu.roll(x, d, 1), 0.0))
    return [v.reshape(n, L).astype(BF16) for v in out]


def toeplitz(c0, c1, later, out, at):
    c0 = pltpu.roll(jnp.broadcast_to(c0, (L, L)), 0, 1, stride=1, stride_axis=0)
    c1 = pltpu.roll(jnp.broadcast_to(c1, (L, L)), 0, 1, stride=1, stride_axis=0)
    out[0:L, at : at + L] = jnp.where(later, 0.0, c1).astype(BF16)
    out[L : 2 * L, at : at + L] = jnp.where(later, c1, c0).astype(BF16)
    out[2 * L : 3 * L, at : at + L] = jnp.where(later, c0, 0.0).astype(BF16)


def kernel(
    n_src, n_rcv, scale,
    traces, mask, filters, slots,
    residual, grad_rcv, grad_src,
    xin, mask_in, filt_in, slots_in,
    xt, x3, x3t, floc, send, raw, recv, res, live,
    m128, mt, fm, f_row, table, tabf, taps, g128, gsnd, hrec, toep, x3m,
    gmsg, parts, mine, land_r, land_s, order_r, order_s,
    stage_sems, s_in, s_x, r_x, s_w, r_w, s_f, r_f, s_g, r_g, s_z, r_z, s_c, r_c, s_h, r_h, s_p, r_p, s_a, r_a, s_b, r_b,
):
    S, R = lax.axis_index("src"), lax.axis_index("rcv")
    rows_p, cols_q = 2 * n_rcv, 2 * n_src
    rows = n_rcv * 16
    (nl, ny, nc), (nx, nh) = digits_of(n_src, n_rcv)
    l, y, c = S // (ny * nc), lax.rem(S // nc, ny), lax.rem(S, nc)
    x, h = R // nh, lax.rem(R, nh)

    def at_src(dl, dy, dc):
        return (lax.rem(l + dl, nl) * ny + lax.rem(y + dy, ny)) * nc + lax.rem(c + dc, nc)

    def at_rcv(dx, dh):
        return lax.rem(x + dx, nx) * nh + lax.rem(h + dh, nh)

    z = [(at_src(a, 0, 0), at_rcv(0, b)) for a in range(nl) for b in range(nh) if a or b]
    xs = [(S, at_rcv(a, 0)) for a in range(1, nx)]
    ys = [(at_src(0, a, 0), R) for a in range(1, ny)]
    cs = [(at_src(0, 0, a), R) for a in range(1, nc)]
    bar = pltpu.get_barrier_semaphore()
    near = z + xs + ys + cs
    for d in near:
        pl.semaphore_signal(bar, inc=1, device_id=d, device_id_type=MESH)
    loads = [
        pltpu.make_async_copy(a, b, s_in.at[i])
        for i, (a, b) in enumerate(
            ((filters, filt_in), (mask, mask_in), (slots, slots_in), (traces, xin))
        )
    ]
    for a in loads:
        a.start()

    def stage(i, group):
        for d in group:
            pl.semaphore_signal(stage_sems.at[i], inc=1, device_id=d, device_id_type=MESH)

    offsets = rcv_offsets(nx, nh)
    n_raw = raw_of(n_rcv)
    to_rcv = [at_rcv(a, b) for a, b in offsets]
    from_rcv = [at_rcv(nx - a, nh - b) for a, b in offsets[:n_raw]]

    m128[...] = jnp.zeros((L, L), F32)
    fm[...] = jnp.zeros(fm.shape, F32)
    g128[...] = jnp.zeros((L, L), F32)
    loads[0].wait()
    f = filt_in[...].astype(F32)
    loads[1].wait()
    m128[0:rows_p, 0:cols_q] = mask_in[...].astype(F32)
    for r in range(n_rcv):
        fm[r, 0:2, :] = f[:, :L]
        fm[r, 2:4, :] = f[:, L:]
        fm[r, 4:6, :] = m128[2 * r : 2 * r + 2, :]

    pl.semaphore_wait(bar, len(near))
    stage(0, xs)
    loads[2].wait()
    loads[3].wait()

    def spread(p, carry):
        for b in range(NB):
            xt[p, pl.ds(b, cols_q, stride=NB), :] = xin[p, :, b * L : (b + 1) * L].astype(F32)
        return carry

    lax.fori_loop(0, rows_p, spread, 0)
    pl.semaphore_wait(stage_sems.at[0], len(xs))

    own8 = pl.ds(pl.multiple_of(R * 8, 8), 8)
    for d in to_rcv[:-1]:
        pltpu.make_async_remote_copy(
            fm.at[d], f_row.at[own8], s_f, r_f, device_id=(S, d), device_id_type=MESH
        ).start()
    stage(1, ys)
    f_row[own8, :] = fm[R]
    for i, d in enumerate(to_rcv[:n_raw]):
        a = xt[2 * d].reshape(n_src, 8, L)
        b = xt[2 * d + 1].reshape(n_src, 8, L)
        raw[i] = swap_middle(a, b)
    mt[...] = jnp.transpose(m128[...])
    pl.semaphore_wait(stage_sems.at[1], len(ys))
    stage(2, cs)
    pl.semaphore_wait(stage_sems.at[2], len(cs))

    def send_raw(group):
        for i in group:
            def step(k, carry):
                s = lax.rem(S + k, n_src)
                pltpu.make_async_remote_copy(
                    raw.at[i, s], recv.at[S, R], s_w, r_w.at[i], device_id=(s, to_rcv[i]), device_id_type=MESH
                ).start()
                return carry

            lax.fori_loop(0, n_src, step, 0)

    n_ahead = min(AHEAD, n_raw)
    send_raw(range(n_ahead))

    wait_bytes(f_row.at[pl.ds(0, (n_rcv - 1) * 8)], r_f)
    for i in range(4):
        table[S, i * n_rcv : (i + 1) * n_rcv, :] = f_row[pl.ds(i, n_rcv, stride=8), :].astype(BF16)

    lines = [at_src(a, 0, 0) for a in range(nl)]
    for d in lines[1:]:
        pltpu.make_async_remote_copy(
            table.at[S], table.at[S], s_z, r_z, device_id=(d, R), device_id_type=MESH
        ).start()
    for i in range(2):
        g128[64 + i * n_rcv : 64 + (i + 1) * n_rcv, :] = f_row[pl.ds(4 + i, n_rcv, stride=8), :]
    gt = jnp.transpose(g128[...])
    for s in range(n_src):
        gsnd[s] = gt[2 * s : 2 * s + 2, :]

    def send_live(k, carry):
        d = lax.rem(S + k, n_src)
        pltpu.make_async_remote_copy(
            gsnd.at[d], hrec.at[S], s_h, r_h, device_id=(d, R), device_id_type=MESH
        ).start()
        return carry

    lax.fori_loop(1, n_src, send_live, 0)

    send_raw(range(n_ahead, n_raw))
    hrec[S] = gsnd[S]
    flip = jnp.where(iota((L, L), 0) + iota((L, L), 1) == L - 1, 1.0, 0.0).astype(BF16)

    def delays(s, carry):
        v3 = delayed(xt[:, pl.ds(pl.multiple_of(s * 8, 8), 8), :])
        for d in range(3):
            at = (2 - d) * L
            x3[s, :, at : at + L] = v3[d]
            x3t[s, at : at + L, :] = lax.dot_general(
                flip, v3[d], (((1,), (1,)), ((), ())), preferred_element_type=F32
            ).astype(BF16)
        return carry

    lax.fori_loop(0, n_src, delays, 0)

    if nl > 1:
        wait_bytes(table.at[pl.ds(0, nl - 1)], r_z)
    for a in range(1, ny):
        for b in lines:
            pltpu.make_async_remote_copy(
                table.at[b], table.at[b], s_g, r_g, device_id=(at_src(0, a, 0), R), device_id_type=MESH
            ).start()
    if nl > 1:
        wait_bytes(table.at[pl.ds(0, nl - 1)], s_z)
    wait_bytes(table.at[pl.ds(0, nl * (ny - 1))], r_g)
    for k in range(1, nc):
        for a in range(nl):
            for b in range(ny):
                t = at_src(a, b, 0)
                pltpu.make_async_remote_copy(
                    table.at[t], table.at[t], s_c, r_c, device_id=(at_src(0, 0, k), R), device_id_type=MESH
                ).start()
    wait_bytes(table.at[pl.ds(0, n_src - nl * ny)], r_c)
    tabf[...] = table[...].astype(F32).reshape(tabf.shape)

    def pick(slot, w):
        st = slots_in[slot]
        at = (st // (2 * n_rcv)) * (4 * n_rcv) + lax.rem(st, 2) * n_rcv + lax.rem(st // 2, n_rcv)
        taps[pl.ds(2 * w, 1), :] = tabf[pl.ds(at, 1), :]
        taps[pl.ds(2 * w + 1, 1), :] = tabf[pl.ds(at + 2 * n_rcv, 1), :]

    def pick_pair(w, carry):
        slot = (w * n_rcv + R) * 2
        pick(slot, 2 * w)
        pick(slot + 1, 2 * w + 1)
        return carry

    lax.fori_loop(0, n_src, pick_pair, 0)
    for i, d in enumerate(from_rcv):
        for p in range(2):
            pick(S * rows_p + 2 * d + p, cols_q + 2 * i + p)

    later = iota((L, L), 1) >= iota((L, L), 0)
    row8 = iota((rows // 8, 8, L), 1)
    q2 = (row8 // NB).reshape(rows, L)
    p2 = lax.rem(iota((rows, L), 0) // (2 * NB), 2)

    def offset_of(i):
        o = n_src - 1 - i
        return lax.rem(o // nc, nl), o // (nc * nl), lax.rem(o, nc)

    def pair_taps(w, out):
        for i in range(2):
            at = 4 * w + 2 * i
            toeplitz(taps[pl.ds(at, 1), :], taps[pl.ds(at + 1, 1), :], later, out, i * L)

    def filter_two(i0, last):
        to = []
        for u in range(2):
            dl, dy, dc = offset_of(i0 + u)
            s = at_src(dl, dy, dc)
            to.append(s)
            pair_taps(s, toep.at[u])
        for u, s in enumerate(to):
            v = jnp.dot(x3[s], toep[u], preferred_element_type=F32)
            v = jnp.where(q2 == 1, v[:, L:], v[:, :L]).astype(BF16)
            floc[s] = v
            v = v.astype(F32).reshape(n_rcv, 2, 8, L)
            send[s] = swap_middle(v[:, 0], v[:, 1])
        for u, s in enumerate(to):
            own = last and u == 1
            for d in to_rcv[n_raw : n_rcv - (1 if own else 0)]:
                pltpu.make_async_remote_copy(
                    send.at[s, d], recv.at[S, R], s_x, r_x.at[i0 + u], device_id=(s, d), device_id_type=MESH
                ).start()

    def filter_step(i, carry):
        filter_two(2 * i, False)
        return carry

    lax.fori_loop(0, n_src // 2 - 1, filter_step, 0)
    filter_two(n_src - 2, True)
    recv[S, R] = send[S, R]

    wait_bytes(hrec.at[pl.ds(0, n_src - 1)], r_h)
    lane = iota((rows, L), 1)
    tile = iota((rows, L), 0) // 16
    pown = lane == 2 * tile + p2
    prec = lane == 64 + q2 * n_rcv + tile
    ones = jnp.where((iota((L, 2 * L), 0) < 64) == (iota((L, 2 * L), 1) < L), 1.0, 0.0).astype(BF16)

    def widen(i, carry):
        for u in range(2):
            s = 2 * i + u
            own = jnp.where(q2 == 0, mt[pl.ds(2 * s, 1), :], mt[pl.ds(2 * s + 1, 1), :])
            other = jnp.where(p2 == 0, hrec[s, 0:1, :], hrec[s, 1:2, :])
            v = jnp.where(pown, own, jnp.where(prec, other, 0.0)).astype(BF16)
            live[s] = jnp.dot(v, ones, preferred_element_type=F32).astype(BF16)
        return carry

    lax.fori_loop(0, n_src // 2, widen, 0)

    for i, d in enumerate(from_rcv):
        wait_bytes(recv.at[0], r_w.at[i])
        v = recv[:, pl.ds(d, 1)].reshape(rows // 8, 8, L).astype(F32)
        v3 = delayed(v)
        for k in range(3):
            x3m[i % 2, :, (2 - k) * L : (3 - k) * L] = v3[k]
        pair_taps(n_src + i, toep.at[i % 2])
        v = jnp.dot(x3m[i % 2], toep[i % 2], preferred_element_type=F32)
        v = jnp.where(p2 == 1, v[:, L:], v[:, :L]).astype(BF16)
        recv[:, pl.ds(d, 1)] = v.reshape(n_src, 1, 16, L)

    reach = iota((L, L), 1) + iota((L, L), 0) >= L - 1

    def lag_pairs(i0, count, last):
        found = []
        for u in range(count):
            dl, dy, dc = offset_of(i0 + u)
            s = at_src(nl - dl, ny - dy, nc - dc)
            wait_bytes(recv.at[0, pl.ds(0, n_rcv - n_raw - (1 if last else 0))], r_x.at[i0 + u])
            found.append(s)
        ms = []
        for s in found:
            diff = floc[s].astype(F32) - recv[s].reshape(rows, L).astype(F32)
            lv = live[s].astype(F32)
            for t in range(2):
                r = lv[:, t * L : (t + 1) * L] * diff
                if t == 0:
                    res[:, pl.ds(pl.multiple_of(s * 8, 8), 8), :] = r.reshape(rows_p, 8, L)
                both = jnp.concatenate([jnp.where(q2 == 0, r, 0.0), jnp.where(q2 == 1, r, 0.0)], axis=1)
                ms.append(jnp.dot(x3t[s], both.astype(BF16), preferred_element_type=F32))
        for u, s in enumerate(found):
            sums = []
            for t in range(2):
                m = ms[2 * u + t]
                for i in range(2):
                    mi = m[:, i * L : (i + 1) * L]
                    m2, m1, m0 = mi[0:L], mi[L : 2 * L], mi[2 * L : 3 * L]
                    for a, b in ((m0, m1), (m1, m2)):
                        skew = pltpu.roll(jnp.where(reach, a, b), 1, 1, stride=1, stride_axis=0)
                        sums.append(jnp.sum(skew, axis=0, keepdims=True))
            msg = jnp.concatenate(sums, axis=0)
            if last:
                parts[S] = msg
            else:
                gmsg[s] = msg
                pltpu.make_async_remote_copy(
                    gmsg.at[s], parts.at[S], s_p, r_p, device_id=(s, R), device_id_type=MESH
                ).start()

    def lag_step(i, carry):
        lag_pairs(2 * i, 2, False)
        return carry

    lax.fori_loop(0, n_src // 2 - 1, lag_step, 0)
    lag_pairs(n_src - 2, 1, False)
    lag_pairs(n_src - 1, 1, True)

    wait_bytes(parts.at[pl.ds(0, n_src - 1)], r_p)
    total = jnp.sum(parts[...], axis=0) * scale
    mine[0] = total[:4]
    mine[1] = total[4:]
    for d in to_rcv[:-1]:
        pltpu.make_async_remote_copy(
            mine.at[1], land_s.at[R], s_b, r_b, device_id=(S, d), device_id_type=MESH
        ).start()

    def send_src(k, carry):
        pltpu.make_async_remote_copy(
            mine.at[0], land_r.at[S], s_a, r_a, device_id=(lax.rem(S + k, n_src), R), device_id_type=MESH
        ).start()
        return carry

    lax.fori_loop(1, n_src, send_src, 0)
    land_r[S] = total[:4]
    land_s[R] = total[4:]

    def gather(p, carry):
        for b in range(NB):
            xin[p, :, b * L : (b + 1) * L] = res[p, pl.ds(b, cols_q, stride=NB), :].astype(BF16)
        return carry

    lax.fori_loop(0, rows_p, gather, 0)
    store = pltpu.make_async_copy(xin, residual, s_in.at[3])
    store.start()
    wait_bytes(f_row.at[pl.ds(0, (n_rcv - 1) * 8)], s_f)
    wait_bytes(table.at[pl.ds(0, nl * (ny - 1))], s_g)
    wait_bytes(table.at[pl.ds(0, n_src - nl * ny)], s_c)
    wait_bytes(hrec.at[pl.ds(0, n_src - 1)], s_h)
    wait_bytes(parts.at[pl.ds(0, n_src - 1)], s_p)
    wait_bytes(raw, s_w)
    for i in range(n_src):
        wait_bytes(recv.at[0, pl.ds(0, n_rcv - n_raw - (1 if i == n_src - 1 else 0))], s_x)
    wait_bytes(land_r.at[pl.ds(0, n_src - 1)], s_a)
    wait_bytes(land_s.at[pl.ds(0, n_rcv - 1)], s_b)
    wait_bytes(land_r.at[pl.ds(0, n_src - 1)], r_a)
    wait_bytes(land_s.at[pl.ds(0, n_rcv - 1)], r_b)
    for i in range(2):
        for k in range(2):
            order_r[k, pl.ds(i, n_src, stride=2), :] = land_r[:, 2 * i + k, :]
            order_s[k, pl.ds(i, n_rcv, stride=2), :] = land_s[:, 2 * i + k, :]
    for k in range(2):
        at = slice(k * L, (k + 1) * L)
        grad_rcv[:, at] = order_r[k]
        grad_src[:, at] = order_s[k]
    store.wait()


def hand_on(a, b, c, x, y, z, buf, buf_r, buf_s, sems):
    parts = buf.shape[0] // 4
    ways = [(a.at[pl.ds(i * parts, parts)], buf.at[pl.ds(i * parts, parts)], x.at[pl.ds(i * parts, parts)]) for i in range(4)]
    ways += [(b, buf_r, y), (c, buf_s, z)]
    loads = [pltpu.make_async_copy(i, m, sems.at[0, k]) for k, (i, m, o) in enumerate(ways)]
    stores = [pltpu.make_async_copy(m, o, sems.at[1, k]) for k, (i, m, o) in enumerate(ways)]
    for copy in loads:
        copy.start()
    for load, store in zip(loads, stores):
        load.wait()
        store.start()
    for copy in stores:
        copy.wait()


def shards(traces, dead_mask, filters, station_of_slot):
    rows_p, cols_q, trace_len = traces.shape
    tap_count = filters.shape[1]
    n_src, n_rcv = lax.axis_size("src"), lax.axis_size("rcv")
    rows = n_rcv * 16
    n_raw = raw_of(n_rcv)
    scale = 1.0 / math.sqrt(rows_p * n_src * trace_len)
    vm = pl.BlockSpec(memory_space=pltpu.VMEM)
    hbm = pl.BlockSpec(memory_space=pltpu.HBM)
    V = pltpu.VMEM
    D = pltpu.SemaphoreType.DMA
    shapes = (
        jax.ShapeDtypeStruct(traces.shape, BF16),
        jax.ShapeDtypeStruct((cols_q, tap_count), F32),
        jax.ShapeDtypeStruct((rows_p, tap_count), F32),
    )
    outs = pl.pallas_call(
        functools.partial(kernel, n_src, n_rcv, scale),
        out_shape=shapes,
        in_specs=[hbm] * 4,
        out_specs=(hbm, vm, vm),
        scratch_shapes=[
            V(traces.shape, BF16),
            V(dead_mask.shape, jnp.int32),
            V(filters.shape, BF16),
            pltpu.SMEM(station_of_slot.shape, jnp.int32),
            V((rows_p, NB * cols_q, L), F32),
            V((n_src, rows, 3 * L), BF16),
            V((n_src, 3 * L, rows), BF16),
            V((n_src, rows, L), BF16),
            V((n_src, n_rcv, 16, L), BF16),
            V((n_raw, n_src, 16, L), BF16),
            V((n_src, n_rcv, 16, L), BF16),
            V((rows_p, NB * cols_q, L), F32),
            V((n_src, rows, 2 * L), BF16),
            V((L, L), F32),
            V((L, L), F32),
            V((n_rcv, 8, L), F32),
            V((n_rcv * 8, L), F32),
            V((n_src, 4 * n_rcv, L), BF16),
            V((n_src * 4 * n_rcv, L), F32),
            V((2 * cols_q + 4 * n_raw, L), F32),
            V((L, L), F32),
            V((n_src, 2, L), F32),
            V((n_src, 2, L), F32),
            V((2, 3 * L, 2 * L), BF16),
            V((2, rows, 3 * L), BF16),
            V((n_src, 8, L), F32),
            V((n_src, 8, L), F32),
            V((2, 4, L), F32),
            V((n_src, 4, L), F32),
            V((n_rcv, 4, L), F32),
            V((2, cols_q, L), F32),
            V((2, rows_p, L), F32),
            pltpu.SemaphoreType.REGULAR((3,)),
            D((4,)), D, D((n_src,)), D, D((n_raw,)),
            D, D, D, D, D, D, D, D, D, D, D, D, D, D, D, D,
        ],
        compiler_params=pltpu.CompilerParams(
            collective_id=0, has_side_effects=True, vmem_limit_bytes=60 << 20
        ),
    )(traces, dead_mask, filters, station_of_slot)
    return pl.pallas_call(
        hand_on,
        out_shape=shapes,
        in_specs=[hbm] * 3,
        out_specs=(hbm,) * 3,
        scratch_shapes=[V(traces.shape, BF16), V(shapes[1].shape, F32), V(shapes[2].shape, F32), D((2, 6))],
    )(*outs)


def solution(mesh):
    placed = (P("src", "rcv", None), P("src", "rcv"), P(("src", "rcv"), None), P())
    return jax.shard_map(
        shards,
        mesh=mesh,
        in_specs=placed,
        out_specs=(P("src", "rcv", None), P("rcv", None), P("src", None)),
        check_vma=False,
    )
```

```python
import functools
import math

import jax
import jax.numpy as jnp
from jax import lax
from jax.experimental import pallas as pl
from jax.experimental.pallas import tpu as pltpu
from jax.sharding import PartitionSpec as P

MESH = pl.DeviceIdType.MESH
F32 = jnp.float32
BF16 = jnp.bfloat16
NB = 4
L = 128
RAW = 7
AHEAD = 4


def digits_of(n_src, n_rcv):
    if (n_src, n_rcv) == (16, 16):
        return (2, 4, 2), (4, 4)
    return (1, n_src // 2, 2), (n_rcv // 2, 2)


def rcv_offsets(nx, nh):
    def far(d):
        return 2 * min(d[1], nh - d[1]), min(d[0], nx - d[0])

    return sorted([(a, b) for a in range(nx) for b in range(nh)], key=far, reverse=True)


def raw_of(n_rcv):
    return n_rcv * RAW // 16


def wait_bytes(ref, sem):
    pltpu.make_async_copy(ref, ref, sem).wait()


def iota(shape, axis):
    return lax.broadcasted_iota(jnp.int32, shape, axis)


def swap_middle(a, b):
    low = iota(a.shape, 1) < 4
    ra, rb = pltpu.roll(a, 4, 1), pltpu.roll(b, 4, 1)
    w0, w1 = jnp.where(low, a, rb), jnp.where(low, ra, b)
    return jnp.concatenate([w0, w1], axis=1).astype(BF16)


def delayed(x):
    block = lax.rem(iota(x.shape, 1), NB)
    n = x.shape[0] * 8
    out = [x]
    for d in (1, 2):
        out.append(jnp.where(block >= d, pltpu.roll(x, d, 1), 0.0))
    return [v.reshape(n, L).astype(BF16) for v in out]


def toeplitz(c0, c1, later, out, at):
    c0 = pltpu.roll(jnp.broadcast_to(c0, (L, L)), 0, 1, stride=1, stride_axis=0)
    c1 = pltpu.roll(jnp.broadcast_to(c1, (L, L)), 0, 1, stride=1, stride_axis=0)
    out[0:L, at : at + L] = jnp.where(later, 0.0, c1).astype(BF16)
    out[L : 2 * L, at : at + L] = jnp.where(later, c1, c0).astype(BF16)
    out[2 * L : 3 * L, at : at + L] = jnp.where(later, c0, 0.0).astype(BF16)


def kernel(
    n_src, n_rcv, scale,
    traces, mask, filters, slots,
    residual, grad_rcv, grad_src,
    xin, mask_in, filt_in, slots_in,
    xt, x3, x3t, floc, send, raw, recv, res, live,
    m128, mt, fm, f_row, table, tabf, taps, g128, gsnd, hrec, toep, x3m,
    gmsg, parts, mine, land_r, land_s, order_r, order_s,
    stage_sems, s_in, s_x, r_x, s_w, r_w, s_f, r_f, s_g, r_g, s_z, r_z, s_c, r_c, s_h, r_h, s_p, r_p, s_a, r_a, s_b, r_b,
):
    S, R = lax.axis_index("src"), lax.axis_index("rcv")
    rows_p, cols_q = 2 * n_rcv, 2 * n_src
    rows = n_rcv * 16
    (nl, ny, nc), (nx, nh) = digits_of(n_src, n_rcv)
    l, y, c = S // (ny * nc), lax.rem(S // nc, ny), lax.rem(S, nc)
    x, h = R // nh, lax.rem(R, nh)

    def at_src(dl, dy, dc):
        return (lax.rem(l + dl, nl) * ny + lax.rem(y + dy, ny)) * nc + lax.rem(c + dc, nc)

    def at_rcv(dx, dh):
        return lax.rem(x + dx, nx) * nh + lax.rem(h + dh, nh)

    z = [(at_src(a, 0, 0), at_rcv(0, b)) for a in range(nl) for b in range(nh) if a or b]
    xs = [(S, at_rcv(a, 0)) for a in range(1, nx)]
    ys = [(at_src(0, a, 0), R) for a in range(1, ny)]
    cs = [(at_src(0, 0, a), R) for a in range(1, nc)]
    bar = pltpu.get_barrier_semaphore()
    near = z + xs + ys + cs
    for d in near:
        pl.semaphore_signal(bar, inc=1, device_id=d, device_id_type=MESH)
    loads = [
        pltpu.make_async_copy(a, b, s_in.at[i])
        for i, (a, b) in enumerate(
            ((filters, filt_in), (mask, mask_in), (slots, slots_in), (traces, xin))
        )
    ]
    for a in loads:
        a.start()

    def stage(i, group):
        for d in group:
            pl.semaphore_signal(stage_sems.at[i], inc=1, device_id=d, device_id_type=MESH)

    offsets = rcv_offsets(nx, nh)
    n_raw = raw_of(n_rcv)
    to_rcv = [at_rcv(a, b) for a, b in offsets]
    from_rcv = [at_rcv(nx - a, nh - b) for a, b in offsets[:n_raw]]

    m128[...] = jnp.zeros((L, L), F32)
    fm[...] = jnp.zeros(fm.shape, F32)
    g128[...] = jnp.zeros((L, L), F32)
    loads[0].wait()
    f = filt_in[...].astype(F32)
    loads[1].wait()
    m128[0:rows_p, 0:cols_q] = mask_in[...].astype(F32)
    for r in range(n_rcv):
        fm[r, 0:2, :] = f[:, :L]
        fm[r, 2:4, :] = f[:, L:]
        fm[r, 4:6, :] = m128[2 * r : 2 * r + 2, :]

    pl.semaphore_wait(bar, len(near))
    stage(0, xs)
    loads[2].wait()
    loads[3].wait()

    def spread(p, carry):
        for b in range(NB):
            xt[p, pl.ds(b, cols_q, stride=NB), :] = xin[p, :, b * L : (b + 1) * L].astype(F32)
        return carry

    lax.fori_loop(0, rows_p, spread, 0)
    pl.semaphore_wait(stage_sems.at[0], len(xs))

    own8 = pl.ds(pl.multiple_of(R * 8, 8), 8)
    for d in to_rcv[:-1]:
        pltpu.make_async_remote_copy(
            fm.at[d], f_row.at[own8], s_f, r_f, device_id=(S, d), device_id_type=MESH
        ).start()
    stage(1, ys)
    f_row[own8, :] = fm[R]
    for i, d in enumerate(to_rcv[:n_raw]):
        a = xt[2 * d].reshape(n_src, 8, L)
        b = xt[2 * d + 1].reshape(n_src, 8, L)
        raw[i] = swap_middle(a, b)
    mt[...] = jnp.transpose(m128[...])
    pl.semaphore_wait(stage_sems.at[1], len(ys))
    stage(2, cs)
    pl.semaphore_wait(stage_sems.at[2], len(cs))

    def send_raw(group):
        for i in group:
            def step(k, carry):
                s = lax.rem(S + k, n_src)
                pltpu.make_async_remote_copy(
                    raw.at[i, s], recv.at[S, R], s_w, r_w.at[i], device_id=(s, to_rcv[i]), device_id_type=MESH
                ).start()
                return carry

            lax.fori_loop(0, n_src, step, 0)

    n_ahead = min(AHEAD, n_raw)
    send_raw(range(n_ahead))

    wait_bytes(f_row.at[pl.ds(0, (n_rcv - 1) * 8)], r_f)
    for i in range(4):
        table[S, i * n_rcv : (i + 1) * n_rcv, :] = f_row[pl.ds(i, n_rcv, stride=8), :].astype(BF16)

    lines = [at_src(a, 0, 0) for a in range(nl)]
    for d in lines[1:]:
        pltpu.make_async_remote_copy(
            table.at[S], table.at[S], s_z, r_z, device_id=(d, R), device_id_type=MESH
        ).start()
    for i in range(2):
        g128[64 + i * n_rcv : 64 + (i + 1) * n_rcv, :] = f_row[pl.ds(4 + i, n_rcv, stride=8), :]
    gt = jnp.transpose(g128[...])
    for s in range(n_src):
        gsnd[s] = gt[2 * s : 2 * s + 2, :]

    def send_live(k, carry):
        d = lax.rem(S + k, n_src)
        pltpu.make_async_remote_copy(
            gsnd.at[d], hrec.at[S], s_h, r_h, device_id=(d, R), device_id_type=MESH
        ).start()
        return carry

    lax.fori_loop(1, n_src, send_live, 0)

    send_raw(range(n_ahead, n_raw))
    hrec[S] = gsnd[S]
    flip = jnp.where(iota((L, L), 0) + iota((L, L), 1) == L - 1, 1.0, 0.0).astype(BF16)

    def delays(s, carry):
        v3 = delayed(xt[:, pl.ds(pl.multiple_of(s * 8, 8), 8), :])
        for d in range(3):
            at = (2 - d) * L
            x3[s, :, at : at + L] = v3[d]
            x3t[s, at : at + L, :] = lax.dot_general(
                flip, v3[d], (((1,), (1,)), ((), ())), preferred_element_type=F32
            ).astype(BF16)
        return carry

    lax.fori_loop(0, n_src, delays, 0)

    if nl > 1:
        wait_bytes(table.at[pl.ds(0, nl - 1)], r_z)
    for a in range(1, ny):
        for b in lines:
            pltpu.make_async_remote_copy(
                table.at[b], table.at[b], s_g, r_g, device_id=(at_src(0, a, 0), R), device_id_type=MESH
            ).start()
    if nl > 1:
        wait_bytes(table.at[pl.ds(0, nl - 1)], s_z)
    wait_bytes(table.at[pl.ds(0, nl * (ny - 1))], r_g)
    for k in range(1, nc):
        for a in range(nl):
            for b in range(ny):
                t = at_src(a, b, 0)
                pltpu.make_async_remote_copy(
                    table.at[t], table.at[t], s_c, r_c, device_id=(at_src(0, 0, k), R), device_id_type=MESH
                ).start()
    wait_bytes(table.at[pl.ds(0, n_src - nl * ny)], r_c)
    tabf[...] = table[...].astype(F32).reshape(tabf.shape)

    def pick(slot, w):
        st = slots_in[slot]
        at = (st // (2 * n_rcv)) * (4 * n_rcv) + lax.rem(st, 2) * n_rcv + lax.rem(st // 2, n_rcv)
        taps[pl.ds(2 * w, 1), :] = tabf[pl.ds(at, 1), :]
        taps[pl.ds(2 * w + 1, 1), :] = tabf[pl.ds(at + 2 * n_rcv, 1), :]

    def pick_pair(w, carry):
        slot = (w * n_rcv + R) * 2
        pick(slot, 2 * w)
        pick(slot + 1, 2 * w + 1)
        return carry

    lax.fori_loop(0, n_src, pick_pair, 0)
    for i, d in enumerate(from_rcv):
        for p in range(2):
            pick(S * rows_p + 2 * d + p, cols_q + 2 * i + p)

    later = iota((L, L), 1) >= iota((L, L), 0)
    row8 = iota((rows // 8, 8, L), 1)
    q2 = (row8 // NB).reshape(rows, L)
    p2 = lax.rem(iota((rows, L), 0) // (2 * NB), 2)

    def offset_of(i):
        o = n_src - 1 - i
        return lax.rem(o // nc, nl), o // (nc * nl), lax.rem(o, nc)

    def pair_taps(w, out):
        for i in range(2):
            at = 4 * w + 2 * i
            toeplitz(taps[pl.ds(at, 1), :], taps[pl.ds(at + 1, 1), :], later, out, i * L)

    def filter_two(i0, last):
        to = []
        for u in range(2):
            dl, dy, dc = offset_of(i0 + u)
            s = at_src(dl, dy, dc)
            to.append(s)
            pair_taps(s, toep.at[u])
        for u, s in enumerate(to):
            v = jnp.dot(x3[s], toep[u], preferred_element_type=F32)
            v = jnp.where(q2 == 1, v[:, L:], v[:, :L]).astype(BF16)
            floc[s] = v
            v = v.astype(F32).reshape(n_rcv, 2, 8, L)
            send[s] = swap_middle(v[:, 0], v[:, 1])
        for u, s in enumerate(to):
            own = last and u == 1
            for d in to_rcv[n_raw : n_rcv - (1 if own else 0)]:
                pltpu.make_async_remote_copy(
                    send.at[s, d], recv.at[S, R], s_x, r_x.at[i0 + u], device_id=(s, d), device_id_type=MESH
                ).start()

    def filter_step(i, carry):
        filter_two(2 * i, False)
        return carry

    lax.fori_loop(0, n_src // 2 - 1, filter_step, 0)
    filter_two(n_src - 2, True)
    recv[S, R] = send[S, R]

    wait_bytes(hrec.at[pl.ds(0, n_src - 1)], r_h)
    lane = iota((rows, L), 1)
    tile = iota((rows, L), 0) // 16
    pown = lane == 2 * tile + p2
    prec = lane == 64 + q2 * n_rcv + tile
    ones = jnp.where((iota((L, 2 * L), 0) < 64) == (iota((L, 2 * L), 1) < L), 1.0, 0.0).astype(BF16)

    def widen(i, carry):
        for u in range(2):
            s = 2 * i + u
            own = jnp.where(q2 == 0, mt[pl.ds(2 * s, 1), :], mt[pl.ds(2 * s + 1, 1), :])
            other = jnp.where(p2 == 0, hrec[s, 0:1, :], hrec[s, 1:2, :])
            v = jnp.where(pown, own, jnp.where(prec, other, 0.0)).astype(BF16)
            live[s] = jnp.dot(v, ones, preferred_element_type=F32).astype(BF16)
        return carry

    lax.fori_loop(0, n_src // 2, widen, 0)

    for i, d in enumerate(from_rcv):
        wait_bytes(recv.at[0], r_w.at[i])
        v = recv[:, pl.ds(d, 1)].reshape(rows // 8, 8, L).astype(F32)
        v3 = delayed(v)
        for k in range(3):
            x3m[i % 2, :, (2 - k) * L : (3 - k) * L] = v3[k]
        pair_taps(n_src + i, toep.at[i % 2])
        v = jnp.dot(x3m[i % 2], toep[i % 2], preferred_element_type=F32)
        v = jnp.where(p2 == 1, v[:, L:], v[:, :L]).astype(BF16)
        recv[:, pl.ds(d, 1)] = v.reshape(n_src, 1, 16, L)

    reach = iota((L, L), 1) + iota((L, L), 0) >= L - 1

    def lag_pairs(i0, count, last):
        found = []
        for u in range(count):
            dl, dy, dc = offset_of(i0 + u)
            s = at_src(nl - dl, ny - dy, nc - dc)
            wait_bytes(recv.at[0, pl.ds(0, n_rcv - n_raw - (1 if last else 0))], r_x.at[i0 + u])
            found.append(s)
        ms = []
        for s in found:
            diff = floc[s].astype(F32) - recv[s].reshape(rows, L).astype(F32)
            lv = live[s].astype(F32)
            for t in range(2):
                r = lv[:, t * L : (t + 1) * L] * diff
                if t == 0:
                    res[:, pl.ds(pl.multiple_of(s * 8, 8), 8), :] = r.reshape(rows_p, 8, L)
                both = jnp.concatenate([jnp.where(q2 == 0, r, 0.0), jnp.where(q2 == 1, r, 0.0)], axis=1)
                ms.append(jnp.dot(x3t[s], both.astype(BF16), preferred_element_type=F32))
        for u, s in enumerate(found):
            sums = []
            for t in range(2):
                m = ms[2 * u + t]
                for i in range(2):
                    mi = m[:, i * L : (i + 1) * L]
                    m2, m1, m0 = mi[0:L], mi[L : 2 * L], mi[2 * L : 3 * L]
                    for a, b in ((m0, m1), (m1, m2)):
                        skew = pltpu.roll(jnp.where(reach, a, b), 1, 1, stride=1, stride_axis=0)
                        sums.append(jnp.sum(skew, axis=0, keepdims=True))
            msg = jnp.concatenate(sums, axis=0)
            if last:
                parts[S] = msg
            else:
                gmsg[s] = msg
                pltpu.make_async_remote_copy(
                    gmsg.at[s], parts.at[S], s_p, r_p, device_id=(s, R), device_id_type=MESH
                ).start()

    def lag_step(i, carry):
        lag_pairs(2 * i, 2, False)
        return carry

    lax.fori_loop(0, n_src // 2 - 1, lag_step, 0)
    lag_pairs(n_src - 2, 1, False)
    lag_pairs(n_src - 1, 1, True)

    wait_bytes(parts.at[pl.ds(0, n_src - 1)], r_p)
    total = jnp.sum(parts[...], axis=0) * scale
    mine[0] = total[:4]
    mine[1] = total[4:]
    for d in to_rcv[:-1]:
        pltpu.make_async_remote_copy(
            mine.at[1], land_s.at[R], s_b, r_b, device_id=(S, d), device_id_type=MESH
        ).start()

    def send_src(k, carry):
        pltpu.make_async_remote_copy(
            mine.at[0], land_r.at[S], s_a, r_a, device_id=(lax.rem(S + k, n_src), R), device_id_type=MESH
        ).start()
        return carry

    lax.fori_loop(1, n_src, send_src, 0)
    land_r[S] = total[:4]
    land_s[R] = total[4:]

    def gather(p, carry):
        for b in range(NB):
            xin[p, :, b * L : (b + 1) * L] = res[p, pl.ds(b, cols_q, stride=NB), :].astype(BF16)
        return carry

    lax.fori_loop(0, rows_p, gather, 0)
    store = pltpu.make_async_copy(xin, residual, s_in.at[3])
    store.start()
    wait_bytes(f_row.at[pl.ds(0, (n_rcv - 1) * 8)], s_f)
    wait_bytes(table.at[pl.ds(0, nl * (ny - 1))], s_g)
    wait_bytes(table.at[pl.ds(0, n_src - nl * ny)], s_c)
    wait_bytes(hrec.at[pl.ds(0, n_src - 1)], s_h)
    wait_bytes(parts.at[pl.ds(0, n_src - 1)], s_p)
    wait_bytes(raw, s_w)
    for i in range(n_src):
        wait_bytes(recv.at[0, pl.ds(0, n_rcv - n_raw - (1 if i == n_src - 1 else 0))], s_x)
    wait_bytes(land_r.at[pl.ds(0, n_src - 1)], s_a)
    wait_bytes(land_s.at[pl.ds(0, n_rcv - 1)], s_b)
    wait_bytes(land_r.at[pl.ds(0, n_src - 1)], r_a)
    wait_bytes(land_s.at[pl.ds(0, n_rcv - 1)], r_b)
    for i in range(2):
        for k in range(2):
            order_r[k, pl.ds(i, n_src, stride=2), :] = land_r[:, 2 * i + k, :]
            order_s[k, pl.ds(i, n_rcv, stride=2), :] = land_s[:, 2 * i + k, :]
    for k in range(2):
        at = slice(k * L, (k + 1) * L)
        grad_rcv[:, at] = order_r[k]
        grad_src[:, at] = order_s[k]
    store.wait()


def hand_on(a, b, c, x, y, z, buf, buf_r, buf_s, sems):
    parts = buf.shape[0] // 4
    ways = [(a.at[pl.ds(i * parts, parts)], buf.at[pl.ds(i * parts, parts)], x.at[pl.ds(i * parts, parts)]) for i in range(4)]
    ways += [(b, buf_r, y), (c, buf_s, z)]
    loads = [pltpu.make_async_copy(i, m, sems.at[0, k]) for k, (i, m, o) in enumerate(ways)]
    stores = [pltpu.make_async_copy(m, o, sems.at[1, k]) for k, (i, m, o) in enumerate(ways)]
    for copy in loads:
        copy.start()
    for load, store in zip(loads, stores):
        load.wait()
        store.start()
    for copy in stores:
        copy.wait()


def shards(traces, dead_mask, filters, station_of_slot):
    rows_p, cols_q, trace_len = traces.shape
    tap_count = filters.shape[1]
    n_src, n_rcv = lax.axis_size("src"), lax.axis_size("rcv")
    rows = n_rcv * 16
    n_raw = raw_of(n_rcv)
    scale = 1.0 / math.sqrt(rows_p * n_src * trace_len)
    vm = pl.BlockSpec(memory_space=pltpu.VMEM)
    hbm = pl.BlockSpec(memory_space=pltpu.HBM)
    V = pltpu.VMEM
    D = pltpu.SemaphoreType.DMA
    shapes = (
        jax.ShapeDtypeStruct(traces.shape, BF16),
        jax.ShapeDtypeStruct((cols_q, tap_count), F32),
        jax.ShapeDtypeStruct((rows_p, tap_count), F32),
    )
    outs = pl.pallas_call(
        functools.partial(kernel, n_src, n_rcv, scale),
        out_shape=shapes,
        in_specs=[hbm] * 4,
        out_specs=(hbm, vm, vm),
        scratch_shapes=[
            V(traces.shape, BF16),
            V(dead_mask.shape, jnp.int32),
            V(filters.shape, BF16),
            pltpu.SMEM(station_of_slot.shape, jnp.int32),
            V((rows_p, NB * cols_q, L), F32),
            V((n_src, rows, 3 * L), BF16),
            V((n_src, 3 * L, rows), BF16),
            V((n_src, rows, L), BF16),
            V((n_src, n_rcv, 16, L), BF16),
            V((n_raw, n_src, 16, L), BF16),
            V((n_src, n_rcv, 16, L), BF16),
            V((rows_p, NB * cols_q, L), F32),
            V((n_src, rows, 2 * L), BF16),
            V((L, L), F32),
            V((L, L), F32),
            V((n_rcv, 8, L), F32),
            V((n_rcv * 8, L), F32),
            V((n_src, 4 * n_rcv, L), BF16),
            V((n_src * 4 * n_rcv, L), F32),
            V((2 * cols_q + 4 * n_raw, L), F32),
            V((L, L), F32),
            V((n_src, 2, L), F32),
            V((n_src, 2, L), F32),
            V((2, 3 * L, 2 * L), BF16),
            V((2, rows, 3 * L), BF16),
            V((n_src, 8, L), F32),
            V((n_src, 8, L), F32),
            V((2, 4, L), F32),
            V((n_src, 4, L), F32),
            V((n_rcv, 4, L), F32),
            V((2, cols_q, L), F32),
            V((2, rows_p, L), F32),
            pltpu.SemaphoreType.REGULAR((3,)),
            D((4,)), D, D((n_src,)), D, D((n_raw,)),
            D, D, D, D, D, D, D, D, D, D, D, D, D, D, D, D,
        ],
        compiler_params=pltpu.CompilerParams(
            collective_id=0, has_side_effects=True, vmem_limit_bytes=60 << 20
        ),
    )(traces, dead_mask, filters, station_of_slot)
    return pl.pallas_call(
        hand_on,
        out_shape=shapes,
        in_specs=[hbm] * 3,
        out_specs=(hbm,) * 3,
        scratch_shapes=[V(traces.shape, BF16), V(shapes[1].shape, F32), V(shapes[2].shape, F32), D((2, 6))],
    )(*outs)


def solution(mesh):
    placed = (P("src", "rcv", None), P("src", "rcv"), P(("src", "rcv"), None), P())
    return jax.shard_map(
        shards,
        mesh=mesh,
        in_specs=placed,
        out_specs=(P("src", "rcv", None), P("rcv", None), P("src", None)),
        check_vma=False,
    )
```
